32 devices in a mesh: groups: 2 (over y), ctx: 16 (over z, x, core).
Axes of the slice: x: 2, y: 2, z: 4, core: 2. Of those that a mesh axis runs over, the one named last changes fastest.
Arguments:
- hidden_in: bfloat16 [4096, 8192], P(('groups', 'ctx')), parts along dimension 0, may hold values from -6 to 6
- queries: bfloat16 [4096, 4096], P(('groups', 'ctx')), parts along dimension 0, may hold values from -5 to 5
- keys: bfloat16 [4096, 512], P(('groups', 'ctx')), parts along dimension 0, may hold values from -5 to 5
- frozen_values: bfloat16 [4096, 512], P(('groups', 'ctx')), parts along dimension 0, may hold values from -6 to 6
- d_out: bfloat16 [4096, 4096], P(('groups', 'ctx')), parts along dimension 0, may hold values from -1.5 to 1.5
- adapter_down: bfloat16 [16, 8192, 16], P(None, 'ctx'), may hold values from -0.0625 to 0.0625
- adapter_up: bfloat16 [16, 8192], P(None, 'ctx'), may hold values from -0.29882812 to 0.29882812
- seg_tiles: int32 [16], P('groups'), parts along dimension 0, may hold values from 1 to 4, as said below
- seg_tenant: int32 [16], P('groups'), parts along dimension 0, may hold values from 0 to 15
Outputs:
- d_queries: bfloat16 [4096, 4096], P(('groups', 'ctx')), parts along dimension 0
- d_keys: bfloat16 [4096, 512], P(('groups', 'ctx')), parts along dimension 0
- d_values: bfloat16 [4096, 512], P(('groups', 'ctx')), parts along dimension 0
- d_adapter_down: float32 [32, 8192, 16], P('groups', 'ctx'), parts along dimension 0
- d_adapter_up: float32 [32, 8192], P('groups', 'ctx'), parts along dimension 0
The draws below stay inside these ranges and needn't reach their ends.
There are 2 independent parts, one for each index of `groups`. The reference program is written for one: setup_inputs(seed, part) draws one part's arguments, and reference() takes and returns one part's arrays. A program takes and returns all parts, laid end to end along the dimension named above; an argument that names none is the same for every part. Nothing has to cross between parts.
Inputs may be any that keep to these rules, and one draw needn't show every extreme that they name: Segment i covers seg_tiles[i] whole tiles of 128 rows; together they cover all 16 tiles, and some segment has exactly 4 tiles.
All inputs are finite; a program needn't handle non-finite values.
Results may differ from the reference program's by a relative error of at most 0.011.
Values may be sent and summed in bfloat16 or wider, within the bound.
A program may use at most 128 MiB of HBM per device.

```python
import math
import jax
import jax.numpy as jnp
import numpy as np
from jax import lax

D = 8192
QUERY_HEADS = 32
KEY_VALUE_HEADS = 4
HEAD_SIZE = 128
R = 16
TILE = 128
SEGMAX = 512
TOK_DEV = 128
ADAPTERS = 16
PACK_TOKENS = 2048
SEGS = 8
KVW = 512
QW = 4096
REACH = 3
N_CTX = 16


def draw_queries(key, part):
    key = jax.random.fold_in(key, 7)
    return jax.random.truncated_normal(key, -5.0, 5.0, (PACK_TOKENS, QUERY_HEADS * HEAD_SIZE), jnp.float32).astype(jnp.bfloat16)


def draw_keys(key, part):
    key = jax.random.fold_in(key, 9)
    return jax.random.truncated_normal(key, -5.0, 5.0, (PACK_TOKENS, KEY_VALUE_HEADS * HEAD_SIZE), jnp.float32).astype(jnp.bfloat16)


def draw_seg_tiles(key, part):
    key = jax.random.fold_in(key, 21)
    longest = SEGMAX // TILE
    triples = 2 * max(1, SEGS // 16)
    pairs = (SEGS - 3 * triples) // 2
    units = triples + pairs
    spread = min(1, longest - 2)
    first_short = (6 - longest) // 2
    second_short = 6 - longest - first_short
    order = jax.random.permutation(jax.random.fold_in(key, 1), units).astype(jnp.int32)
    is_triple = (order < triples).astype(jnp.int32)
    unit_sizes = 2 + is_triple
    unit_starts = (jnp.cumsum(unit_sizes) - unit_sizes).astype(jnp.int32)
    pattern = jax.random.randint(jax.random.fold_in(key, 2), (units,), 0, 3, dtype=jnp.int32)
    pattern = jnp.where(order == 0, 1, pattern).astype(jnp.int32)
    pair_shift = jax.random.randint(jax.random.fold_in(key, 3), (units,), -spread, spread + 1, dtype=jnp.int32)
    slot = jnp.arange(3, dtype=jnp.int32)[None, :]
    short_rank = slot - (slot > pattern[:, None]).astype(jnp.int32)
    short_value = jnp.where(short_rank == 0, first_short, second_short).astype(jnp.int32)
    triple_value = jnp.where(slot == pattern[:, None], longest, short_value).astype(jnp.int32)
    pair_value = jnp.where(slot == 0, 2 + pair_shift[:, None], 2 - pair_shift[:, None]).astype(jnp.int32)
    values = jnp.where(is_triple[:, None] == 1, triple_value, pair_value).astype(jnp.int32)
    target = unit_starts[:, None] + slot
    target = jnp.where((is_triple[:, None] == 0) & (slot == 2), SEGS, target).astype(jnp.int32)
    segment_index = jnp.arange(SEGS, dtype=jnp.int32)
    match = (target.reshape(-1)[None, :] == segment_index[:, None]).astype(jnp.int32)
    return jnp.sum(match * values.reshape(-1)[None, :], axis=1).astype(jnp.int32)


def with_ends(values, key, least, high):
    longest = values.shape.index(max(values.shape))
    spots = []
    for shift in (0, 1):
        where = [jax.random.randint(jax.random.fold_in(key, axis), (), 0, length) for axis, length in enumerate(values.shape)]
        where[longest] = (where[longest] + shift) % values.shape[longest]
        spots.append(tuple(where))
    return values.at[spots[0]].set(least).at[spots[1]].set(high)


def block_levels(key, dims, split, smallest, top_value):
    level = 1.0
    for position, blocks in split:
        steps = jax.random.uniform(jax.random.fold_in(jax.random.fold_in(key, 6), position), (blocks,), jnp.float32, smallest / len(split), top_value / len(split))
        level = level * jnp.repeat(jnp.exp(steps), dims[position] // blocks).reshape((-1,) + (1,) * (len(dims) - 1 - position))
    return level


def rank_bounds(amount, lean):
    loads = [(1 << 20) // math.isqrt(rank ** lean) + 1 for rank in range(1, amount + 1)]
    scale = 1 + sum(loads) // (1 << 30)
    return np.cumsum(np.array([max(1, weight // scale) for weight in loads]))


def skewed_ids(stream_key, shape, count, slope):
    listing = rank_bounds(count, slope)
    pick = jax.random.randint(jax.random.fold_in(stream_key, 1), shape, 0, int(listing[count - 1]))
    grade = jnp.searchsorted(jnp.asarray(listing, jnp.int32), pick, side="right")
    return jax.random.permutation(jax.random.fold_in(stream_key, 2), count)[grade].astype(jnp.int32)


def gaussian(own_key, extent, deviation, bound, split=(), kind=jnp.bfloat16):
    drawn = jax.random.normal(own_key, extent, jnp.float32) * deviation
    if len(split) > 0:
        drawn = block_levels(own_key, extent, split, -0.22, 0.18) * drawn
    return jnp.clip(drawn, min=-bound, max=bound).astype(kind)


def setup_inputs(seed: int = 0, part: int = 0) -> dict:
    streams_of = jax.random.split(jax.random.key(seed), 10)
    part_keys = jax.random.split(jax.random.fold_in(streams_of[9], part), 10)
    return {
        "hidden_in": gaussian(part_keys[0], (PACK_TOKENS, D), 1.0, 6.0, ((0, 16),)),
        "queries": draw_queries(jax.random.fold_in(jax.random.fold_in(streams_of[9], part), 71), part),
        "keys": draw_keys(jax.random.fold_in(jax.random.fold_in(streams_of[9], part), 71), part),
        "frozen_values": gaussian(part_keys[3], (PACK_TOKENS, KVW), 1.0, 6.0, ((0, 16),)),
        "d_out": gaussian(part_keys[4], (PACK_TOKENS, QW), 0.25, 1.5, ((0, 16),)),
        "adapter_down": gaussian(streams_of[5], (ADAPTERS, D, R), D ** -0.5, 0.0625, ((1, 16),)),
        "adapter_up": gaussian(streams_of[6], (ADAPTERS, R * KVW), 0.05, 0.29882812, ((1, 16),)),
        "seg_tiles": draw_seg_tiles(jax.random.fold_in(jax.random.fold_in(streams_of[9], part), 71), part),
        "seg_tenant": with_ends(skewed_ids(part_keys[8], (SEGS,), ADAPTERS, 2), jax.random.fold_in(part_keys[8], 3), 0, ADAPTERS - 1).astype(jnp.int32),
    }


ADAPTER_SCALE = 2.0
NEG_BIG = -1e+30

def expand_heads(array):
    return lax.optimization_barrier(array).astype(jnp.float32)

def tile_segments(seg_tiles, total_tiles):
    segment_ends = jnp.cumsum(seg_tiles.astype(jnp.int32)).astype(jnp.int32)
    tile_index = jnp.arange(total_tiles, dtype=jnp.int32)
    return lax.optimization_barrier(jnp.sum((segment_ends[None, :] <= tile_index[:, None]).astype(jnp.int32), axis=1)).astype(jnp.int32)

def window_grads(rows_of_query, rows_of_key, rows_of_value, gradient_rows, allowed):
    count_of_query = rows_of_query.shape[0]
    window_length = rows_of_key.shape[0]
    group_width = QUERY_HEADS // KEY_VALUE_HEADS
    score_scale = 1.0 / jnp.sqrt(jnp.float32(HEAD_SIZE))
    heads_of_query = expand_heads(rows_of_query).reshape(count_of_query, KEY_VALUE_HEADS, group_width, HEAD_SIZE)
    gradient_heads = expand_heads(gradient_rows).reshape(count_of_query, KEY_VALUE_HEADS, group_width, HEAD_SIZE)
    heads_of_key = expand_heads(rows_of_key).reshape(window_length, KEY_VALUE_HEADS, HEAD_SIZE)
    heads_of_value = expand_heads(rows_of_value).reshape(window_length, KEY_VALUE_HEADS, HEAD_SIZE)
    query_list = []
    key_collection = []
    value_collection = []
    for key_value_head in range(KEY_VALUE_HEADS):
        query_part = heads_of_query[:, key_value_head]
        grad_part = gradient_heads[:, key_value_head]
        key_part = heads_of_key[:, key_value_head]
        value_part = heads_of_value[:, key_value_head]
        scores = jnp.einsum('tgd,wd->gtw', query_part, key_part) * score_scale
        scores = jnp.where(allowed[None], scores, NEG_BIG)
        row_top = lax.optimization_barrier(jnp.max(scores, axis=-1, keepdims=True))
        weights = jnp.where(allowed[None], jnp.exp(scores - row_top), 0.0)
        prob_full = weights / lax.optimization_barrier(jnp.sum(weights, axis=-1, keepdims=True))
        prob_half = prob_full.astype(jnp.bfloat16)
        attended = jnp.einsum('gtw,wd->tgd', expand_heads(prob_half), value_part).astype(jnp.bfloat16)
        row_delta = lax.optimization_barrier(jnp.sum(grad_part * expand_heads(attended), axis=-1)).T
        d_prob = jnp.einsum('tgd,wd->gtw', grad_part, value_part)
        d_score = (prob_full * (d_prob - row_delta[:, :, None]) * score_scale).astype(jnp.bfloat16)
        query_list.append(jnp.einsum('gtw,wd->tgd', expand_heads(d_score), key_part))
        key_collection.append(jnp.einsum('gtw,tgd->wd', expand_heads(d_score), query_part))
        value_collection.append(jnp.einsum('gtw,tgd->wd', expand_heads(prob_half), grad_part))
    d_query = jnp.stack(query_list, axis=1).reshape(count_of_query, QUERY_HEADS * HEAD_SIZE)
    key_gradient = jnp.stack(key_collection, axis=1).reshape(window_length, KEY_VALUE_HEADS * HEAD_SIZE)
    value_gradient = jnp.stack(value_collection, axis=1).reshape(window_length, KEY_VALUE_HEADS * HEAD_SIZE)
    return (d_query, key_gradient, value_gradient)

def reference(hidden_in, queries, keys, frozen_values, d_out, adapter_down, adapter_up, seg_tiles, seg_tenant):
    total_tiles = PACK_TOKENS // TILE
    key_value_width = KEY_VALUE_HEADS * HEAD_SIZE
    tile_segment = tile_segments(seg_tiles, total_tiles)
    tenant_per_tile = jnp.take(seg_tenant, tile_segment).astype(jnp.int32)
    input_tiles = hidden_in.reshape(total_tiles, TILE, D)
    up_all = adapter_up.reshape(ADAPTERS, R, key_value_width)

    def adapter_down_proj(element):
        x_tile, tenant = element
        down_mat = lax.dynamic_index_in_dim(adapter_down, tenant, 0, keepdims=False)
        return jnp.dot(expand_heads(x_tile), expand_heads(down_mat), preferred_element_type=jnp.float32).astype(jnp.bfloat16)
    low_rank_product = lax.map(adapter_down_proj, (input_tiles, tenant_per_tile))
    up_matrix_tiles = jnp.take(up_all, tenant_per_tile, axis=0)
    adapter_term = jnp.einsum('mqw,mws->mqs', expand_heads(low_rank_product), expand_heads(up_matrix_tiles)).reshape(PACK_TOKENS, key_value_width)
    value_matrix = (expand_heads(frozen_values) + ADAPTER_SCALE * adapter_term).astype(jnp.bfloat16)
    pad_rows = REACH * TOK_DEV
    window_length = (REACH + 1) * TOK_DEV
    token_segment = jnp.repeat(tile_segment, TILE).astype(jnp.int32)
    key_pad = jnp.concatenate([jnp.zeros((pad_rows, key_value_width), jnp.bfloat16), keys], axis=0)
    value_pad = jnp.concatenate([jnp.zeros((pad_rows, key_value_width), jnp.bfloat16), value_matrix], axis=0)
    segment_pad = jnp.concatenate([jnp.full((pad_rows,), -1, jnp.int32), token_segment], axis=0)
    key_place = jnp.arange(window_length, dtype=jnp.int32)
    query_place = pad_rows + jnp.arange(TOK_DEV, dtype=jnp.int32)

    def block(carry, block_start):
        key_total, value_total = carry
        rows_of_query = lax.dynamic_slice_in_dim(queries, block_start, TOK_DEV, 0)
        gradient_rows = lax.dynamic_slice_in_dim(d_out, block_start, TOK_DEV, 0)
        rows_of_key = lax.dynamic_slice_in_dim(key_pad, block_start, window_length, 0)
        rows_of_value = lax.dynamic_slice_in_dim(value_pad, block_start, window_length, 0)
        segment_rows = lax.dynamic_slice_in_dim(segment_pad, block_start, window_length, 0)
        query_segment = segment_rows[pad_rows:]
        allowed = (query_segment[:, None] == segment_rows[None, :]) & (key_place[None, :] <= query_place[:, None])
        d_query, key_gradient, value_gradient = window_grads(rows_of_query, rows_of_key, rows_of_value, gradient_rows, allowed)
        key_total = lax.dynamic_update_slice_in_dim(key_total, lax.dynamic_slice_in_dim(key_total, block_start, window_length, 0) + key_gradient, block_start, 0)
        value_total = lax.dynamic_update_slice_in_dim(value_total, lax.dynamic_slice_in_dim(value_total, block_start, window_length, 0) + value_gradient, block_start, 0)
        return ((key_total, value_total), d_query)
    block_starts = jnp.arange(N_CTX, dtype=jnp.int32) * TOK_DEV
    start_totals = (jnp.zeros((pad_rows + PACK_TOKENS, key_value_width), jnp.float32), jnp.zeros((pad_rows + PACK_TOKENS, key_value_width), jnp.float32))
    (key_total, value_total), query_blocks = lax.scan(block, start_totals, block_starts)
    d_queries = query_blocks.reshape(PACK_TOKENS, QUERY_HEADS * HEAD_SIZE).astype(jnp.bfloat16)
    d_keys = key_total[pad_rows:].astype(jnp.bfloat16)
    d_values = value_total[pad_rows:].astype(jnp.bfloat16)
    tiles_of_value = d_values.reshape(total_tiles, TILE, key_value_width)
    low_rank_gradient = (ADAPTER_SCALE * jnp.einsum('ihx,idx->ihd', expand_heads(tiles_of_value), expand_heads(up_matrix_tiles))).astype(jnp.bfloat16)
    up_gradient = ADAPTER_SCALE * jnp.einsum('wmh,wmi->whi', expand_heads(low_rank_product), expand_heads(tiles_of_value))
    d_adapter_up = jax.ops.segment_sum(up_gradient.reshape(total_tiles, R * key_value_width), tenant_per_tile, num_segments=ADAPTERS)

    def add_down(total, element):
        x_tile, grad_tile, tenant = element
        term = jnp.dot(expand_heads(x_tile).T, expand_heads(grad_tile), preferred_element_type=jnp.float32)
        current = lax.dynamic_index_in_dim(total, tenant, 0, keepdims=False)
        return (lax.dynamic_update_index_in_dim(total, current + term, tenant, 0), None)
    d_adapter_down, _ = lax.scan(add_down, jnp.zeros((ADAPTERS, D, R), jnp.float32), (input_tiles, low_rank_gradient, tenant_per_tile))
    return (d_queries, d_keys, d_values, d_adapter_down, d_adapter_up)
```

```python
import functools

import jax
import jax.numpy as jnp
from jax import lax
from jax.experimental import pallas as pl
from jax.experimental.pallas import tpu as pltpu
from jax.sharding import PartitionSpec as P

HEAD_SIZE = 128
R = 16
TILE = 128
SEGMAX = 512
ADAPTER_SCALE = 2.0
NEG_BIG = -1e30
LOG2E = 1.4426950408889634
NT = (((1,), (1,)), ((), ()))
F32 = jnp.float32
BF16 = jnp.bfloat16


def dot(a, b):
    return jnp.dot(a, b, preferred_element_type=F32)


def dot_nt(a, b):
    return lax.dot_general(a, b, NT, preferred_element_type=F32)


def kernel(
    n, reach, seg_tiles, seg_tenant, hidden_hbm, q_hbm, keys_hbm, frozen_hbm, do_hbm, down_hbm, up_ref,
    dq_hbm, dk_ref, dv_ref, gd_ref, gu_ref,
    hidden, q, do, frozen, down, kwin, vwin, upf, send_a, recv_a, pbuf, dsbuf, dqv, tri,
    dv_own, dv_send, dv_recv, dk_own, dk_send, dk_recv, send_g, recv_g, pick, ten,
    load_sem, dq_sem, k_s, k_r, v_s, v_r, a_s, a_r, dv_s, dv_r, dk_s, dk_r, g_s, g_r,
):
    me = lax.axis_index("ctx")
    adapters, _, piece = down.shape
    up_piece = upf.shape[1]
    up_lanes = min(up_piece, 128)
    up_rows = up_piece // up_lanes
    kvw = frozen.shape[1]
    groups = kvw // HEAD_SIZE
    gw = q.shape[1] // groups
    heads = gw // HEAD_SIZE
    per_row = kvw // up_lanes
    segs = seg_tiles.shape[0]
    window = (reach + 1) * TILE
    scale = HEAD_SIZE ** -0.5

    pairs = (
        (keys_hbm, kwin.at[0]), (down_hbm, down), (q_hbm, q), (do_hbm, do),
        (hidden_hbm, hidden), (frozen_hbm, frozen),
    )
    loads = [pltpu.make_async_copy(a, b, load_sem.at[i]) for i, (a, b) in enumerate(pairs)]
    for load in loads:
        load.start()

    barrier = pltpu.get_barrier_semaphore()

    def greet(i, carry):
        pl.semaphore_signal(
            barrier, inc=1, device_id={"ctx": lax.rem(me + i, n)}, device_id_type=pl.DeviceIdType.MESH
        )
        return carry

    lax.fori_loop(1, n, greet, 0)

    ends = []
    total = jnp.int32(0)
    for i in range(segs):
        total = total + seg_tiles[i]
        ends.append(total)

    def segment(j):
        s = jnp.int32(0)
        for end in ends:
            s = s + (end <= j).astype(jnp.int32)
        return s

    def note(j, carry):
        ten[j] = seg_tenant[jnp.minimum(segment(j), segs - 1)]
        return carry

    lax.fori_loop(0, n, note, 0)
    my_segment = segment(me)
    bias = [None]
    for d in range(1, reach + 1):
        same = jnp.logical_and(me >= d, segment(me - d) == my_segment)
        bias.append(jnp.where(same, jnp.float32(0), jnp.float32(NEG_BIG)))
    w_place = lax.broadcasted_iota(jnp.int32, (TILE, TILE), 0)
    t_place = lax.broadcasted_iota(jnp.int32, (TILE, TILE), 1)
    tri[...] = jnp.where(w_place <= t_place, 0.0, NEG_BIG).astype(F32)
    upf[...] = up_ref[...].astype(F32)

    for d in range(1, reach + 1):
        @pl.when(me < d)
        def _():
            kwin[d] = jnp.zeros((TILE, kvw), BF16)
            vwin[d] = jnp.zeros((TILE, kvw), BF16)

        @pl.when(me + d >= n)
        def _():
            for g in range(groups):
                dv_recv[g, d - 1] = jnp.zeros((TILE, HEAD_SIZE), BF16)
                dk_recv[g, d - 1] = jnp.zeros((TILE, HEAD_SIZE), BF16)

    def forward(win, d, ss, rs):
        return pltpu.make_async_remote_copy(
            src_ref=win.at[0], dst_ref=win.at[d], send_sem=ss.at[d - 1], recv_sem=rs.at[d - 1],
            device_id={"ctx": lax.rem(me + d, n)}, device_id_type=pl.DeviceIdType.MESH,
        )

    def backward(src, dst, g, d, ss, rs):
        at = g * reach + d - 1
        return pltpu.make_async_remote_copy(
            src_ref=src.at[g, d - 1], dst_ref=dst.at[g, d - 1], send_sem=ss.at[at], recv_sem=rs.at[at],
            device_id={"ctx": lax.rem(me + n - d, n)}, device_id_type=pl.DeviceIdType.MESH,
        )

    def rows(j):
        return pl.ds(pl.multiple_of(j * R, R), R)

    def scatter(src, dst, peer, ss, rs):
        return pltpu.make_async_remote_copy(
            src_ref=src.at[rows(peer)], dst_ref=dst.at[rows(me)], send_sem=ss.at[peer], recv_sem=rs.at[me],
            device_id={"ctx": peer}, device_id_type=pl.DeviceIdType.MESH,
        )

    def arrived(dst, source, ss, rs):
        return pltpu.make_async_remote_copy(
            src_ref=dst.at[rows(source)], dst_ref=dst.at[rows(source)], send_sem=ss.at[source],
            recv_sem=rs.at[source], device_id={"ctx": source}, device_id_type=pl.DeviceIdType.MESH,
        )

    def wait_arrivals(dst, ss, rs):
        def one(i, carry):
            arrived(dst, lax.rem(me + i, n), ss, rs).wait_recv()
            return carry

        lax.fori_loop(1, n, one, 0)

    def wait_sends(src, dst, ss, rs):
        def one(i, carry):
            scatter(src, dst, lax.rem(me + i, n), ss, rs).wait_send()
            return carry

        lax.fori_loop(1, n, one, 0)

    row_id = lax.broadcasted_iota(jnp.int32, (R, up_lanes), 0)

    def factors(j):
        tenant = ten[j]
        row = upf[pl.ds(tenant, 1), :]
        tail = jnp.zeros((R, up_lanes), F32)
        for k in range(up_rows):
            tail = jnp.where(row_id == k, row[:, k * up_lanes:(k + 1) * up_lanes], tail)
        return down[tenant], tail.astype(BF16)

    loads[0].wait()
    loads[1].wait()
    pl.semaphore_wait(barrier, n - 1)
    for d in range(1, reach + 1):
        @pl.when(me + d < n)
        def _():
            forward(kwin, d, k_s, k_r).start()

    def give(i, carry):
        peer = lax.rem(me + i, n)
        mat, tail = factors(peer)
        send_a[rows(peer), 0:piece] = mat
        send_a[rows(peer), piece:piece + up_lanes] = tail
        scatter(send_a, recv_a, peer, a_s, a_r).start()
        return carry

    lax.fori_loop(1, n, give, 0)
    mat, tail = factors(me)
    recv_a[rows(me), 0:piece] = mat
    recv_a[rows(me), piece:piece + up_lanes] = tail

    col = lax.broadcasted_iota(jnp.int32, (1, n * R), 1)
    col_tile = jnp.right_shift(col, 4)
    col_rank = jnp.bitwise_and(col, R - 1)
    col_tenant = jnp.zeros((1, n * R), jnp.int32)
    for j in range(n):
        col_tenant = jnp.where(col_tile == j, ten[j], col_tenant)
    blocks = adapters // 16
    for b in range(blocks):
        line = lax.broadcasted_iota(jnp.int32, (16 * R, n * R), 0)
        hit = jnp.logical_and(
            col_tenant == b * 16 + jnp.right_shift(line, 4), col_rank == jnp.bitwise_and(line, R - 1)
        )
        pick[b * 16 * R:(b + 1) * 16 * R, :] = jnp.where(hit, 1.0, 0.0).astype(BF16)

    loads[2].wait()
    loads[3].wait()
    for d in range(1, reach + 1):
        @pl.when(me >= d)
        def _():
            forward(kwin, d, k_s, k_r).wait_recv()

    def lanes(g, width):
        return pl.ds(pl.multiple_of(g * width, width), width)

    def stack(ref, g):
        part = ref[:, lanes(g, gw)]
        return jnp.concatenate([part[:, h * HEAD_SIZE:(h + 1) * HEAD_SIZE] for h in range(heads)], axis=0)

    def first(g, carry):
        kg = kwin[:, :, lanes(g, HEAD_SIZE)].reshape(window, HEAD_SIZE)
        qg = q[:, lanes(g, gw)]
        for h in range(heads):
            s = dot_nt(kg, qg[:, h * HEAD_SIZE:(h + 1) * HEAD_SIZE])
            parts = [s[0:TILE] + tri[...]]
            for d in range(1, reach + 1):
                parts.append(s[d * TILE:(d + 1) * TILE] + bias[d])
            s = jnp.concatenate(parts, axis=0)
            top = jnp.max(s, axis=0, keepdims=True)
            e = jnp.exp2((s - top) * (scale * LOG2E))
            inv = 1.0 / jnp.sum(e, axis=0, keepdims=True)
            pbuf[g, :, h * HEAD_SIZE:(h + 1) * HEAD_SIZE] = (e * inv).astype(BF16)
        dv = dot(pbuf[g], stack(do, g))
        dv_own[:, lanes(g, HEAD_SIZE)] = dv[0:TILE]
        for d in range(1, reach + 1):
            dv_send[g, d - 1] = dv[d * TILE:(d + 1) * TILE].astype(BF16)

            @pl.when(me >= d)
            def _():
                backward(dv_send, dv_recv, g, d, dv_s, dv_r).start()
        return carry

    lax.fori_loop(0, groups, first, 0)

    loads[4].wait()
    loads[5].wait()
    wait_arrivals(recv_a, a_s, a_r)
    per = max(1, 512 // piece)
    low_t = jnp.zeros((R, TILE), F32)
    for c in range(0, n, per):
        mats = [recv_a[j * R:(j + 1) * R, 0:piece] for j in range(c, c + per)]
        mats = mats[0] if per == 1 else jnp.concatenate(mats, axis=1)
        low_t = low_t + dot_nt(mats, hidden[:, c * piece:(c + per) * piece])
    low_half = low_t.astype(BF16)
    rank = lax.broadcasted_iota(jnp.int32, (R, n * R), 0)
    ups = []
    for k in range(per_row):
        hit = jnp.logical_and(col_rank < up_rows, col_tile * up_rows + col_rank == rank * per_row + k)
        ups.append(dot(jnp.where(hit, 1.0, 0.0).astype(BF16), recv_a[:, piece:piece + up_lanes]))
    up = jnp.concatenate(ups, axis=1)
    up_half = up.astype(BF16)
    low = jnp.concatenate([low_t, jnp.zeros((TILE - R, TILE), F32)], axis=0).T.astype(BF16)
    up_tall = jnp.concatenate([up, jnp.zeros((TILE - R, kvw), F32)], axis=0).astype(BF16)
    vwin[0] = (frozen[...].astype(F32) + ADAPTER_SCALE * dot(low, up_tall)).astype(BF16)
    for d in range(1, reach + 1):
        @pl.when(me + d < n)
        def _():
            forward(vwin, d, v_s, v_r).start()

    def gather_back(own, send, recv, out, ss, rs):
        for d in range(1, reach + 1):
            @pl.when(me + d < n)
            def _():
                for g in range(groups):
                    backward(send, recv, g, d, ss, rs).wait_recv()
        for g in range(groups):
            acc = own[:, g * HEAD_SIZE:(g + 1) * HEAD_SIZE]
            for d in range(1, reach + 1):
                acc = acc + recv[g, d - 1].astype(F32)
            out[:, g * HEAD_SIZE:(g + 1) * HEAD_SIZE] = acc.astype(BF16)

    gather_back(dv_own, dv_send, dv_recv, dv_ref, dv_s, dv_r)
    dv = dv_ref[...]
    grad_t = (ADAPTER_SCALE * dot_nt(up_half, dv)).astype(BF16)
    up_grad = ADAPTER_SCALE * dot(low_half, dv)
    for j in range(n):
        send_g[j * R:(j + 1) * R, 0:piece] = dot(grad_t, hidden[:, j * piece:(j + 1) * piece]).astype(BF16)
        tail = jnp.zeros((R, up_lanes), F32)
        for k in range(up_rows):
            r, c = divmod(j * up_rows + k, per_row)
            tail = jnp.where(row_id == k, up_grad[r:r + 1, c * up_lanes:(c + 1) * up_lanes], tail)
        send_g[j * R:(j + 1) * R, piece:piece + up_lanes] = tail.astype(BF16)

        @pl.when(me != j)
        def _():
            scatter(send_g, recv_g, j, g_s, g_r).start()

    recv_g[rows(me), :] = send_g[rows(me), :]

    for d in range(1, reach + 1):
        @pl.when(me >= d)
        def _():
            forward(vwin, d, v_s, v_r).wait_recv()

    def dq_out(g):
        return pltpu.make_async_copy(dqv.at[g], dq_hbm.at[:, lanes(g, gw)], dq_sem.at[g])

    def second(g, carry):
        kg = kwin[:, :, lanes(g, HEAD_SIZE)].reshape(window, HEAD_SIZE)
        vg = vwin[:, :, lanes(g, HEAD_SIZE)].reshape(window, HEAD_SIZE)
        dog = do[:, lanes(g, gw)]
        for h in range(heads):
            at = slice(h * HEAD_SIZE, (h + 1) * HEAD_SIZE)
            dp = dot_nt(vg, dog[:, at])
            p = pbuf[g, :, at].astype(F32)
            delta = jnp.sum(p * dp, axis=0, keepdims=True)
            dsbuf[:, at] = (p * ((dp - delta) * scale)).astype(BF16)
        ds = dsbuf[...]
        dk = dot(ds, stack(q, g))
        dk_own[:, lanes(g, HEAD_SIZE)] = dk[0:TILE]
        for d in range(1, reach + 1):
            dk_send[g, d - 1] = dk[d * TILE:(d + 1) * TILE].astype(BF16)

            @pl.when(me >= d)
            def _():
                backward(dk_send, dk_recv, g, d, dk_s, dk_r).start()
        dq_t = dot(kg.astype(F32).T.astype(BF16), dsbuf[...])
        for h in range(heads):
            at = slice(h * HEAD_SIZE, (h + 1) * HEAD_SIZE)
            dqv[g, :, at] = dq_t[:, at].T.astype(BF16)
        dq_out(g).start()
        return carry

    lax.fori_loop(0, groups, second, 0)

    wait_arrivals(recv_g, g_s, g_r)
    line = lax.broadcasted_iota(jnp.int32, (16, n * R), 0)
    for b in range(blocks):
        out = dot(pick[b * 16 * R:(b + 1) * 16 * R, :], recv_g[:, 0:piece])
        gd_ref[b * 16:(b + 1) * 16] = out.reshape(16, R, piece)
        for k in range(up_rows):
            hit = jnp.logical_and(col_tenant == b * 16 + line, col_rank == k)
            gu_ref[b * 16:(b + 1) * 16, k * up_lanes:(k + 1) * up_lanes] = dot(
                jnp.where(hit, 1.0, 0.0).astype(BF16), recv_g[:, piece:piece + up_lanes]
            )
    gather_back(dk_own, dk_send, dk_recv, dk_ref, dk_s, dk_r)

    for g in range(groups):
        dq_out(g).wait()
    for d in range(1, reach + 1):
        @pl.when(me + d < n)
        def _():
            forward(kwin, d, k_s, k_r).wait_send()
            forward(vwin, d, v_s, v_r).wait_send()

        @pl.when(me >= d)
        def _():
            for g in range(groups):
                backward(dv_send, dv_recv, g, d, dv_s, dv_r).wait_send()
                backward(dk_send, dk_recv, g, d, dk_s, dk_r).wait_send()

    wait_sends(send_a, recv_a, a_s, a_r)
    wait_sends(send_g, recv_g, g_s, g_r)


def per_device(
    hidden_in, queries, keys, frozen_values, d_out, adapter_down, adapter_up, seg_tiles, seg_tenant
):
    n = lax.axis_size("ctx")
    row_count, d_model = hidden_in.shape
    reach = (SEGMAX - TILE) // row_count
    adapters, piece, _ = adapter_down.shape
    up_piece = adapter_up.shape[1]
    kvw = keys.shape[1]
    qw = queries.shape[1]
    groups = kvw // HEAD_SIZE
    gw = qw // groups
    window = (reach + 1) * row_count
    wide = piece + min(up_piece, 128)
    vmem = pl.BlockSpec(memory_space=pltpu.VMEM)
    smem = pl.BlockSpec(memory_space=pltpu.SMEM)
    hbm = pl.BlockSpec(memory_space=pl.ANY)
    sem = pltpu.SemaphoreType.DMA
    terms = pltpu.VMEM((groups, reach, row_count, HEAD_SIZE), BF16)
    own = pltpu.VMEM((row_count, kvw), F32)
    a2a = pltpu.VMEM((n * R, wide), BF16)
    d_queries, d_keys, d_values, grad_down, grad_up = pl.pallas_call(
        functools.partial(kernel, n, reach),
        out_shape=(
            jax.ShapeDtypeStruct((row_count, qw), BF16),
            jax.ShapeDtypeStruct((row_count, kvw), BF16),
            jax.ShapeDtypeStruct((row_count, kvw), BF16),
            jax.ShapeDtypeStruct((adapters, R, piece), F32),
            jax.ShapeDtypeStruct((adapters, up_piece), F32),
        ),
        in_specs=[smem, smem, hbm, hbm, hbm, hbm, hbm, hbm, vmem],
        out_specs=(hbm, vmem, vmem, vmem, vmem),
        scratch_shapes=[
            pltpu.VMEM((row_count, d_model), BF16),
            pltpu.VMEM((row_count, qw), BF16),
            pltpu.VMEM((row_count, qw), BF16),
            pltpu.VMEM((row_count, kvw), BF16),
            pltpu.VMEM((adapters, R, piece), BF16),
            pltpu.VMEM((reach + 1, row_count, kvw), BF16),
            pltpu.VMEM((reach + 1, row_count, kvw), BF16),
            pltpu.VMEM((adapters, up_piece), F32),
            a2a,
            a2a,
            pltpu.VMEM((groups, window, gw), BF16),
            pltpu.VMEM((window, gw), BF16),
            pltpu.VMEM((groups, row_count, gw), BF16),
            pltpu.VMEM((TILE, TILE), F32),
            own, terms, terms,
            own, terms, terms,
            a2a,
            a2a,
            pltpu.VMEM((adapters * R, n * R), BF16),
            pltpu.SMEM((n,), jnp.int32),
            sem((6,)),
            sem((groups,)),
            sem((reach,)), sem((reach,)), sem((reach,)), sem((reach,)),
            sem((n,)), sem((n,)),
            sem((groups * reach,)), sem((groups * reach,)),
            sem((groups * reach,)), sem((groups * reach,)),
            sem((n,)), sem((n,)),
        ],
        compiler_params=pltpu.CompilerParams(
            collective_id=0, has_side_effects=True, vmem_limit_bytes=48 * 1024 * 1024
        ),
    )(
        seg_tiles, seg_tenant, hidden_in, queries, keys, frozen_values, d_out,
        jnp.swapaxes(adapter_down, 1, 2), adapter_up,
    )
    return (d_queries, d_keys, d_values, jnp.swapaxes(grad_down, 1, 2), grad_up)


def solution(mesh):
    placed = (
        P(("groups", "ctx"), None),
        P(("groups", "ctx"), None),
        P(("groups", "ctx"), None),
        P(("groups", "ctx"), None),
        P(("groups", "ctx"), None),
        P(None, "ctx", None),
        P(None, "ctx"),
        P("groups"),
        P("groups"),
    )
    return jax.shard_map(
        per_device,
        mesh=mesh,
        in_specs=placed,
        out_specs=(
            P(("groups", "ctx"), None),
            P(("groups", "ctx"), None),
            P(("groups", "ctx"), None),
            P("groups", "ctx", None),
            P("groups", "ctx"),
        ),
        check_vma=False,
    )
```

```python
import functools

import jax
import jax.numpy as jnp
from jax import lax
from jax.experimental import pallas as pl
from jax.experimental.pallas import tpu as pltpu
from jax.sharding import PartitionSpec as P

HEAD_SIZE = 128
R = 16
TILE = 128
SEGMAX = 512
ADAPTER_SCALE = 2.0
NEG_BIG = -1e30
LOG2E = 1.4426950408889634
NT = (((1,), (1,)), ((), ()))
F32 = jnp.float32
BF16 = jnp.bfloat16


def dot(a, b):
    return jnp.dot(a, b, preferred_element_type=F32)


def dot_nt(a, b):
    return lax.dot_general(a, b, NT, preferred_element_type=F32)


def kernel(
    n, reach, tiles_hbm, tenant_hbm, hidden_hbm, q_hbm, keys_hbm, frozen_hbm, do_hbm, down_hbm, up_hbm,
    dq_hbm, dk_ref, dv_ref, gd_ref, gu_ref,
    seg_tiles, seg_tenant, up_in, hidden, q, do, down, kwin, fwin, lwin, vwin, upf, send_a, recv_a, pbuf, dsbuf, dqv, tri,
    dv_buf, dk_buf, send_g, recv_g, pick, ten,
    load_sem, dq_sem, k_s, k_r, f_s, f_r, l_s, l_r, a_s, a_r, dv_s, dv_r, dk_s, dk_r, g_s, g_r,
):
    me = lax.axis_index("ctx")
    odd = lax.rem(me, 2)
    partner = me + 1 - 2 * odd
    adapters, _, piece = down.shape
    up_piece = upf.shape[1]
    up_lanes = min(up_piece, 128)
    up_rows = up_piece // up_lanes
    kvw = kwin.shape[2]
    groups = kvw // HEAD_SIZE
    gw = q.shape[1] // groups
    heads = gw // HEAD_SIZE
    per_row = kvw // up_lanes
    segs = seg_tiles.shape[0]
    window = (reach + 1) * TILE
    scale = HEAD_SIZE ** -0.5

    pairs = (
        (keys_hbm, kwin.at[0]), (down_hbm, down), (q_hbm, q), (do_hbm, do),
        (hidden_hbm, hidden), (frozen_hbm, fwin.at[0]),
        (tiles_hbm, seg_tiles), (tenant_hbm, seg_tenant), (up_hbm, up_in),
    )
    loads = [pltpu.make_async_copy(a, b, load_sem.at[i]) for i, (a, b) in enumerate(pairs)]
    for i in (6, 7, 0, 8, 1, 2, 3, 4, 5):
        loads[i].start()

    barrier = pltpu.get_barrier_semaphore()

    def greet(i, carry):
        pl.semaphore_signal(
            barrier, inc=1, device_id={"ctx": lax.rem(me + i, n)}, device_id_type=pl.DeviceIdType.MESH
        )
        return carry

    lax.fori_loop(1, n, greet, 0)

    loads[6].wait()
    loads[7].wait()
    ends = []
    total = jnp.int32(0)
    for i in range(segs):
        total = total + seg_tiles[i]
        ends.append(total)

    def segment(j):
        s = jnp.int32(0)
        for end in ends:
            s = s + (end <= j).astype(jnp.int32)
        return s

    def note(j, carry):
        ten[j] = seg_tenant[jnp.minimum(segment(j), segs - 1)]
        return carry

    lax.fori_loop(0, n, note, 0)
    my_segment = segment(me)
    bias = [None]
    for d in range(1, reach + 1):
        same = jnp.logical_and(me >= d, segment(me - d) == my_segment)
        bias.append(jnp.where(same, jnp.float32(0), jnp.float32(NEG_BIG)))
    w_place = lax.broadcasted_iota(jnp.int32, (TILE, TILE), 0)
    t_place = lax.broadcasted_iota(jnp.int32, (TILE, TILE), 1)
    tri[...] = jnp.where(w_place <= t_place, 0.0, NEG_BIG).astype(F32)
    loads[8].wait()
    upf[...] = up_in[...].astype(F32)

    for d in range(1, reach + 1):
        @pl.when(me < d)
        def _():
            kwin[d] = jnp.zeros((TILE, kvw), BF16)
            fwin[d] = jnp.zeros((TILE, kvw), BF16)
            lwin[d] = jnp.zeros((R, TILE), BF16)

    def clear(ref):
        ref[...] = jnp.zeros(ref.shape, ref.dtype)

    @pl.when(me + 2 >= n)
    def _():
        clear(dv_buf[6])
        clear(dk_buf[6])

    straight = jnp.logical_or(odd == 0, me + 3 < n)

    @pl.when(jnp.logical_not(straight))
    def _():
        clear(dv_buf[7])
        clear(dk_buf[7])

    def remote(src, dst, ss, rs, peer):
        return pltpu.make_async_remote_copy(
            src_ref=src, dst_ref=dst, send_sem=ss, recv_sem=rs,
            device_id={"ctx": peer}, device_id_type=pl.DeviceIdType.MESH,
        )

    def near(win, ss, rs):
        return remote(win.at[0], win.at[1], ss.at[0], rs.at[0], partner)

    def across(win, ss, rs):
        return remote(win.at[0], win.at[2], ss.at[1], rs.at[1], lax.rem(me + 2, n))

    def far(win, ss, rs):
        return remote(win.at[0], win.at[3], ss.at[2], rs.at[2], lax.rem(me + 3, n))

    def pass_on(win, ss, rs):
        at = 3 - 2 * odd
        return remote(win.at[2], win.at[at], ss.at[3], rs.at[at - 1], partner)

    far_too = jnp.logical_and(odd == 1, me + 3 < n)

    def spread(win, ss, rs):
        @pl.when(me + 2 < n)
        def _():
            across(win, ss, rs).start()

        @pl.when(far_too)
        def _():
            far(win, ss, rs).start()

        @pl.when(odd == 0)
        def _():
            near(win, ss, rs).start()

    def relay(win, ss, rs):
        @pl.when(me >= 2)
        def _():
            across(win, ss, rs).wait_recv()
            pass_on(win, ss, rs).start()

    def settle(win, ss, rs):
        @pl.when(me >= 1)
        def _():
            near(win, ss, rs).wait_recv()

        @pl.when(me >= 3)
        def _():
            far(win, ss, rs).wait_recv()

    def spread_sent(win, ss, rs):
        @pl.when(me + 2 < n)
        def _():
            across(win, ss, rs).wait_send()

        @pl.when(far_too)
        def _():
            far(win, ss, rs).wait_send()

        @pl.when(odd == 0)
        def _():
            near(win, ss, rs).wait_send()

        @pl.when(me >= 2)
        def _():
            pass_on(win, ss, rs).wait_send()

    def meet(buf, ss, rs, g):
        return remote(buf[2].at[g], buf[5].at[g], ss.at[0, g], rs.at[0, g], partner)

    def back(buf, ss, rs, g):
        return remote(buf[4].at[g], buf[6].at[g], ss.at[1, g], rs.at[1, g], lax.rem(me + n - 2, n))

    def direct(buf, ss, rs, g):
        return remote(buf[3].at[g], buf[7].at[g], ss.at[2, g], rs.at[2, g], lax.rem(me + n - 3 + 2 * odd, n))

    has_direct = jnp.logical_or(odd == 1, me >= 3)

    def send_terms(buf, ss, rs, g, terms):
        own, mid = buf[0], buf[1]
        one, two, three = (terms[d * TILE:(d + 1) * TILE] for d in (1, 2, 3))
        own[g] = terms[0:TILE]
        mid[g] = two
        buf[2][g] = jnp.where(odd == 1, three, one).astype(BF16)
        buf[3][g] = jnp.where(odd == 1, one, three).astype(BF16)

        @pl.when(me >= 2)
        def _():
            meet(buf, ss, rs, g).start()

        @pl.when(has_direct)
        def _():
            direct(buf, ss, rs, g).start()

    def finish_terms(buf, ss, rs, g):
        meet(buf, ss, rs, g).wait_recv()
        buf[4][g] = (buf[1][g] + buf[5][g].astype(F32)).astype(BF16)
        back(buf, ss, rs, g).start()

    def gather_back(buf, out, ss, rs):
        for g in range(groups):
            @pl.when(straight)
            def _():
                direct(buf, ss, rs, g).wait_recv()

            @pl.when(me + 2 < n)
            def _():
                back(buf, ss, rs, g).wait_recv()

            acc = buf[0][g] + buf[6][g].astype(F32) + buf[7][g].astype(F32)
            out[:, g * HEAD_SIZE:(g + 1) * HEAD_SIZE] = acc.astype(BF16)

    def terms_sent(buf, ss, rs):
        for g in range(groups):
            @pl.when(me >= 2)
            def _():
                meet(buf, ss, rs, g).wait_send()
                back(buf, ss, rs, g).wait_send()

            @pl.when(has_direct)
            def _():
                direct(buf, ss, rs, g).wait_send()

    def low_copy(d):
        return remote(lwin.at[0], lwin.at[d], l_s.at[d - 1], l_r.at[d - 1], lax.rem(me + d, n))

    def rows(j):
        return pl.ds(pl.multiple_of(j * R, R), R)

    def scatter(src, dst, peer, ss, rs):
        return pltpu.make_async_remote_copy(
            src_ref=src.at[rows(peer)], dst_ref=dst.at[rows(me)], send_sem=ss.at[peer], recv_sem=rs.at[me],
            device_id={"ctx": peer}, device_id_type=pl.DeviceIdType.MESH,
        )

    def arrived(dst, source, ss, rs):
        return pltpu.make_async_remote_copy(
            src_ref=dst.at[rows(source)], dst_ref=dst.at[rows(source)], send_sem=ss.at[source],
            recv_sem=rs.at[source], device_id={"ctx": source}, device_id_type=pl.DeviceIdType.MESH,
        )

    def wait_arrivals(dst, ss, rs):
        def one(i, carry):
            arrived(dst, lax.rem(me + i, n), ss, rs).wait_recv()
            return carry

        lax.fori_loop(1, n, one, 0)

    def wait_sends(src, dst, ss, rs):
        def one(i, carry):
            scatter(src, dst, lax.rem(me + i, n), ss, rs).wait_send()
            return carry

        lax.fori_loop(1, n, one, 0)

    row_id = lax.broadcasted_iota(jnp.int32, (R, up_lanes), 0)

    def factors(j):
        tenant = ten[j]
        row = upf[pl.ds(tenant, 1), :]
        tail = jnp.zeros((R, up_lanes), F32)
        for k in range(up_rows):
            tail = jnp.where(row_id == k, row[:, k * up_lanes:(k + 1) * up_lanes], tail)
        return down[tenant], tail.astype(BF16)

    loads[0].wait()
    loads[1].wait()
    pl.semaphore_wait(barrier, n - 1)
    spread(kwin, k_s, k_r)

    def give(i, carry):
        peer = lax.rem(me + i, n)
        mat, tail = factors(peer)
        send_a[rows(peer), 0:piece] = mat
        send_a[rows(peer), piece:piece + up_lanes] = tail
        scatter(send_a, recv_a, peer, a_s, a_r).start()
        return carry

    lax.fori_loop(1, n, give, 0)
    mat, tail = factors(me)
    recv_a[rows(me), 0:piece] = mat
    recv_a[rows(me), piece:piece + up_lanes] = tail
    loads[5].wait()
    spread(fwin, f_s, f_r)
    relay(kwin, k_s, k_r)

    col = lax.broadcasted_iota(jnp.int32, (1, n * R), 1)
    col_tile = jnp.right_shift(col, 4)
    col_rank = jnp.bitwise_and(col, R - 1)
    col_tenant = jnp.zeros((1, n * R), jnp.int32)
    for j in range(n):
        col_tenant = jnp.where(col_tile == j, ten[j], col_tenant)
    blocks = adapters // 16
    for b in range(blocks):
        line = lax.broadcasted_iota(jnp.int32, (16 * R, n * R), 0)
        hit = jnp.logical_and(
            col_tenant == b * 16 + jnp.right_shift(line, 4), col_rank == jnp.bitwise_and(line, R - 1)
        )
        pick[b * 16 * R:(b + 1) * 16 * R, :] = jnp.where(hit, 1.0, 0.0).astype(BF16)

    loads[2].wait()
    loads[3].wait()
    settle(kwin, k_s, k_r)

    def lanes(g, width):
        return pl.ds(pl.multiple_of(g * width, width), width)

    def stack(ref, g):
        part = ref[:, lanes(g, gw)]
        return jnp.concatenate([part[:, h * HEAD_SIZE:(h + 1) * HEAD_SIZE] for h in range(heads)], axis=0)

    def first(g, carry):
        kg = kwin[:, :, lanes(g, HEAD_SIZE)].reshape(window, HEAD_SIZE)
        qg = q[:, lanes(g, gw)]
        for h in range(heads):
            s = dot_nt(kg, qg[:, h * HEAD_SIZE:(h + 1) * HEAD_SIZE])
            parts = [s[0:TILE] + tri[...]]
            for d in range(1, reach + 1):
                parts.append(s[d * TILE:(d + 1) * TILE] + bias[d])
            s = jnp.concatenate(parts, axis=0)
            top = jnp.max(s, axis=0, keepdims=True)
            e = jnp.exp2((s - top) * (scale * LOG2E))
            inv = 1.0 / jnp.sum(e, axis=0, keepdims=True)
            pbuf[g, :, h * HEAD_SIZE:(h + 1) * HEAD_SIZE] = (e * inv).astype(BF16)
        dv = dot(pbuf[g], stack(do, g))
        send_terms(dv_buf, dv_s, dv_r, g, dv)

        @pl.when(jnp.logical_and(g >= 1, me >= 2))
        def _():
            finish_terms(dv_buf, dv_s, dv_r, g - 1)
        return carry

    lax.fori_loop(0, groups, first, 0)

    @pl.when(me >= 2)
    def _():
        finish_terms(dv_buf, dv_s, dv_r, groups - 1)
    relay(fwin, f_s, f_r)

    loads[4].wait()
    wait_arrivals(recv_a, a_s, a_r)
    per = max(1, 512 // piece)
    low_t = jnp.zeros((R, TILE), F32)
    for c in range(0, n, per):
        mats = [recv_a[j * R:(j + 1) * R, 0:piece] for j in range(c, c + per)]
        mats = mats[0] if per == 1 else jnp.concatenate(mats, axis=1)
        low_t = low_t + dot_nt(mats, hidden[:, c * piece:(c + per) * piece])
    low_half = low_t.astype(BF16)
    rank = lax.broadcasted_iota(jnp.int32, (R, n * R), 0)
    ups = []
    for k in range(per_row):
        hit = jnp.logical_and(col_rank < up_rows, col_tile * up_rows + col_rank == rank * per_row + k)
        ups.append(dot(jnp.where(hit, 1.0, 0.0).astype(BF16), recv_a[:, piece:piece + up_lanes]))
    up = jnp.concatenate(ups, axis=1)
    up_half = up.astype(BF16)
    up_tall = jnp.concatenate([up, jnp.zeros((TILE - R, kvw), F32)], axis=0).astype(BF16)
    lwin[0] = low_half
    for d in range(1, reach + 1):
        @pl.when(me + d < n)
        def _():
            low_copy(d).start()

    gather_back(dv_buf, dv_ref, dv_s, dv_r)
    dv = dv_ref[...]
    grad_t = (ADAPTER_SCALE * dot_nt(up_half, dv)).astype(BF16)
    up_grad = ADAPTER_SCALE * dot(low_half, dv)
    for j in range(n):
        send_g[j * R:(j + 1) * R, 0:piece] = dot(grad_t, hidden[:, j * piece:(j + 1) * piece]).astype(BF16)
        tail = jnp.zeros((R, up_lanes), F32)
        for k in range(up_rows):
            r, c = divmod(j * up_rows + k, per_row)
            tail = jnp.where(row_id == k, up_grad[r:r + 1, c * up_lanes:(c + 1) * up_lanes], tail)
        send_g[j * R:(j + 1) * R, piece:piece + up_lanes] = tail.astype(BF16)

        @pl.when(me != j)
        def _():
            scatter(send_g, recv_g, j, g_s, g_r).start()

    recv_g[rows(me), :] = send_g[rows(me), :]

    settle(fwin, f_s, f_r)
    for d in range(1, reach + 1):
        @pl.when(me >= d)
        def _():
            low_copy(d).wait_recv()

    for d in range(reach + 1):
        low = jnp.concatenate([lwin[d].astype(F32), jnp.zeros((TILE - R, TILE), F32)], axis=0).T
        vwin[d] = (fwin[d].astype(F32) + ADAPTER_SCALE * dot(low.astype(BF16), up_tall)).astype(BF16)

    def dq_out(g):
        return pltpu.make_async_copy(dqv.at[g], dq_hbm.at[:, lanes(g, gw)], dq_sem.at[g])

    def second(g, carry):
        kg = kwin[:, :, lanes(g, HEAD_SIZE)].reshape(window, HEAD_SIZE)
        vg = vwin[:, :, lanes(g, HEAD_SIZE)].reshape(window, HEAD_SIZE)
        dog = do[:, lanes(g, gw)]
        for h in range(heads):
            at = slice(h * HEAD_SIZE, (h + 1) * HEAD_SIZE)
            dp = dot_nt(vg, dog[:, at])
            p = pbuf[g, :, at].astype(F32)
            delta = jnp.sum(p * dp, axis=0, keepdims=True)
            dsbuf[:, at] = (p * ((dp - delta) * scale)).astype(BF16)
        ds = dsbuf[...]
        dk = dot(ds, stack(q, g))
        send_terms(dk_buf, dk_s, dk_r, g, dk)

        @pl.when(jnp.logical_and(g >= 1, me >= 2))
        def _():
            finish_terms(dk_buf, dk_s, dk_r, g - 1)
        dq_t = dot(kg.astype(F32).T.astype(BF16), dsbuf[...])
        for h in range(heads):
            at = slice(h * HEAD_SIZE, (h + 1) * HEAD_SIZE)
            dqv[g, :, at] = dq_t[:, at].T.astype(BF16)
        dq_out(g).start()
        return carry

    lax.fori_loop(0, groups, second, 0)

    @pl.when(me >= 2)
    def _():
        finish_terms(dk_buf, dk_s, dk_r, groups - 1)

    wait_arrivals(recv_g, g_s, g_r)
    line = lax.broadcasted_iota(jnp.int32, (16, n * R), 0)
    for b in range(blocks):
        out = dot(pick[b * 16 * R:(b + 1) * 16 * R, :], recv_g[:, 0:piece])
        gd_ref[b * 16:(b + 1) * 16] = out.reshape(16, R, piece)
        for k in range(up_rows):
            hit = jnp.logical_and(col_tenant == b * 16 + line, col_rank == k)
            gu_ref[b * 16:(b + 1) * 16, k * up_lanes:(k + 1) * up_lanes] = dot(
                jnp.where(hit, 1.0, 0.0).astype(BF16), recv_g[:, piece:piece + up_lanes]
            )
    gather_back(dk_buf, dk_ref, dk_s, dk_r)

    for g in range(groups):
        dq_out(g).wait()
    for d in range(1, reach + 1):
        @pl.when(me + d < n)
        def _():
            low_copy(d).wait_send()
    spread_sent(kwin, k_s, k_r)
    spread_sent(fwin, f_s, f_r)
    terms_sent(dv_buf, dv_s, dv_r)
    terms_sent(dk_buf, dk_s, dk_r)
    wait_sends(send_a, recv_a, a_s, a_r)
    wait_sends(send_g, recv_g, g_s, g_r)


def flush(*refs):
    ins, outs, held, sems = refs[0:5], refs[5:10], refs[10:15], refs[15]
    loads = [pltpu.make_async_copy(ins[i], held[i], sems.at[i]) for i in range(5)]
    stores = [pltpu.make_async_copy(held[i], outs[i], sems.at[5 + i]) for i in range(5)]
    for load in loads:
        load.start()
    for load, store in zip(loads, stores):
        load.wait()
        store.start()
    for store in stores:
        store.wait()


def per_device(
    hidden_in, queries, keys, frozen_values, d_out, adapter_down, adapter_up, seg_tiles, seg_tenant
):
    n = lax.axis_size("ctx")
    row_count, d_model = hidden_in.shape
    reach = (SEGMAX - TILE) // row_count
    adapters, piece, _ = adapter_down.shape
    up_piece = adapter_up.shape[1]
    kvw = keys.shape[1]
    qw = queries.shape[1]
    groups = kvw // HEAD_SIZE
    gw = qw // groups
    window = (reach + 1) * row_count
    wide = piece + min(up_piece, 128)
    vmem = pl.BlockSpec(memory_space=pltpu.VMEM)
    hbm = pl.BlockSpec(memory_space=pltpu.HBM)
    anywhere = pl.BlockSpec(memory_space=pl.ANY)
    sem = pltpu.SemaphoreType.DMA
    block = (groups, row_count, HEAD_SIZE)
    terms = [pltpu.VMEM(block, F32)] * 2 + [pltpu.VMEM(block, BF16)] * 6
    a2a = pltpu.VMEM((n * R, wide), BF16)
    results = pl.pallas_call(
        functools.partial(kernel, n, reach),
        out_shape=(
            jax.ShapeDtypeStruct((row_count, qw), BF16),
            jax.ShapeDtypeStruct((row_count, kvw), BF16),
            jax.ShapeDtypeStruct((row_count, kvw), BF16),
            jax.ShapeDtypeStruct((adapters, R, piece), F32),
            jax.ShapeDtypeStruct((adapters, up_piece), F32),
        ),
        in_specs=[hbm] * 9,
        out_specs=(anywhere, vmem, vmem, vmem, vmem),
        scratch_shapes=[
            pltpu.SMEM(seg_tiles.shape, jnp.int32),
            pltpu.SMEM(seg_tenant.shape, jnp.int32),
            pltpu.VMEM((adapters, up_piece), BF16),
            pltpu.VMEM((row_count, d_model), BF16),
            pltpu.VMEM((row_count, qw), BF16),
            pltpu.VMEM((row_count, qw), BF16),
            pltpu.VMEM((adapters, R, piece), BF16),
            pltpu.VMEM((reach + 1, row_count, kvw), BF16),
            pltpu.VMEM((reach + 1, row_count, kvw), BF16),
            pltpu.VMEM((reach + 1, R, row_count), BF16),
            pltpu.VMEM((reach + 1, row_count, kvw), BF16),
            pltpu.VMEM((adapters, up_piece), F32),
            a2a,
            a2a,
            pltpu.VMEM((groups, window, gw), BF16),
            pltpu.VMEM((window, gw), BF16),
            pltpu.VMEM((groups, row_count, gw), BF16),
            pltpu.VMEM((TILE, TILE), F32),
            terms, terms,
            a2a,
            a2a,
            pltpu.VMEM((adapters * R, n * R), BF16),
            pltpu.SMEM((n,), jnp.int32),
            sem((9,)),
            sem((groups,)),
            sem((4,)), sem((3,)), sem((4,)), sem((3,)),
            sem((3,)), sem((3,)),
            sem((n,)), sem((n,)),
            sem((3, groups)), sem((3, groups)),
            sem((3, groups)), sem((3, groups)),
            sem((n,)), sem((n,)),
        ],
        compiler_params=pltpu.CompilerParams(
            collective_id=0, has_side_effects=True, vmem_limit_bytes=64 * 1024 * 1024
        ),
    )(
        seg_tiles, seg_tenant, hidden_in, queries, keys, frozen_values, d_out,
        jnp.swapaxes(adapter_down, 1, 2), adapter_up,
    )
    d_queries, d_keys, d_values, grad_down, grad_up = pl.pallas_call(
        flush,
        out_shape=tuple(jax.ShapeDtypeStruct(x.shape, x.dtype) for x in results),
        in_specs=[anywhere] * 5,
        out_specs=(hbm,) * 5,
        scratch_shapes=[pltpu.VMEM(x.shape, x.dtype) for x in results] + [sem((10,))],
        compiler_params=pltpu.CompilerParams(vmem_limit_bytes=64 * 1024 * 1024),
    )(*results)
    return (d_queries, d_keys, d_values, jnp.swapaxes(grad_down, 1, 2), grad_up)


def solution(mesh):
    placed = (
        P(("groups", "ctx"), None),
        P(("groups", "ctx"), None),
        P(("groups", "ctx"), None),
        P(("groups", "ctx"), None),
        P(("groups", "ctx"), None),
        P(None, "ctx", None),
        P(None, "ctx"),
        P("groups"),
        P("groups"),
    )
    return jax.shard_map(
        per_device,
        mesh=mesh,
        in_specs=placed,
        out_specs=(
            P(("groups", "ctx"), None),
            P(("groups", "ctx"), None),
            P(("groups", "ctx"), None),
            P("groups", "ctx", None),
            P("groups", "ctx"),
        ),
        check_vma=False,
    )
```

```python
import functools

import jax
import jax.numpy as jnp
from jax import lax
from jax.experimental import pallas as pl
from jax.experimental.pallas import tpu as pltpu
from jax.sharding import PartitionSpec as P

HEAD_SIZE = 128
R = 16
TILE = 128
SEGMAX = 512
ADAPTER_SCALE = 2.0
NEG_BIG = -1e30
LOG2E = 1.4426950408889634
NT = (((1,), (1,)), ((), ()))
F32 = jnp.float32
BF16 = jnp.bfloat16


def dot(a, b):
    return jnp.dot(a, b, preferred_element_type=F32)


def dot_nt(a, b):
    return lax.dot_general(a, b, NT, preferred_element_type=F32)


def kernel(
    n, reach, tiles_hbm, tenant_hbm, hidden_hbm, q_hbm, keys_hbm, frozen_hbm, do_hbm, down_hbm, up_hbm,
    dq_hbm, dk_ref, dv_ref, gd_ref, gu_ref,
    seg_tiles, seg_tenant, up_in, hidden, q, do, down, kwin, fwin, lwin, vwin, upf, send_a, recv_a, pbuf, dqv, tri,
    dv_buf, dk_buf, send_g, recv_g, pick, ten,
    load_sem, dq_sem, k_s, k_r, f_s, f_r, l_s, l_r, a_s, a_r, dv_s, dv_r, dk_s, dk_r, g_s, g_r,
):
    me = lax.axis_index("ctx")
    odd = lax.rem(me, 2)
    partner = me + 1 - 2 * odd
    adapters, _, piece = down.shape
    up_piece = upf.shape[1]
    up_lanes = min(up_piece, 128)
    up_rows = up_piece // up_lanes
    kvw = kwin.shape[2]
    groups = kvw // HEAD_SIZE
    gw = q.shape[1] // groups
    heads = gw // HEAD_SIZE
    per_row = kvw // up_lanes
    segs = seg_tiles.shape[0]
    window = (reach + 1) * TILE
    scale = HEAD_SIZE ** -0.5

    pairs = (
        (keys_hbm, kwin.at[0]), (down_hbm, down), (q_hbm, q), (do_hbm, do),
        (hidden_hbm, hidden), (frozen_hbm, fwin.at[0]),
        (tiles_hbm, seg_tiles), (tenant_hbm, seg_tenant), (up_hbm, up_in),
    )
    loads = [pltpu.make_async_copy(a, b, load_sem.at[i]) for i, (a, b) in enumerate(pairs)]
    for i in (6, 7, 0, 8, 1, 2, 3, 4, 5):
        loads[i].start()

    barrier = pltpu.get_barrier_semaphore()

    def greet(i, carry):
        pl.semaphore_signal(
            barrier, inc=1, device_id={"ctx": lax.rem(me + i, n)}, device_id_type=pl.DeviceIdType.MESH
        )
        return carry

    lax.fori_loop(1, n, greet, 0)

    loads[6].wait()
    loads[7].wait()
    ends = []
    total = jnp.int32(0)
    for i in range(segs):
        total = total + seg_tiles[i]
        ends.append(total)

    def segment(j):
        s = jnp.int32(0)
        for end in ends:
            s = s + (end <= j).astype(jnp.int32)
        return s

    def note(j, carry):
        ten[j] = seg_tenant[jnp.minimum(segment(j), segs - 1)]
        return carry

    lax.fori_loop(0, n, note, 0)
    my_segment = segment(me)
    bias = [None]
    for d in range(1, reach + 1):
        same = jnp.logical_and(me >= d, segment(me - d) == my_segment)
        bias.append(jnp.where(same, jnp.float32(0), jnp.float32(NEG_BIG)))
    w_place = lax.broadcasted_iota(jnp.int32, (TILE, TILE), 0)
    t_place = lax.broadcasted_iota(jnp.int32, (TILE, TILE), 1)
    tri[...] = jnp.where(w_place <= t_place, 0.0, NEG_BIG).astype(F32)
    loads[8].wait()
    upf[...] = up_in[...].astype(F32)

    for d in range(1, reach + 1):
        @pl.when(me < d)
        def _():
            kwin[d] = jnp.zeros((TILE, kvw), BF16)
            fwin[d] = jnp.zeros((TILE, kvw), BF16)
            lwin[d] = jnp.zeros((R, TILE), BF16)

    def clear(ref):
        ref[...] = jnp.zeros(ref.shape, ref.dtype)

    @pl.when(me + 2 >= n)
    def _():
        clear(dv_buf[6])
        clear(dk_buf[6])

    straight = jnp.logical_or(odd == 0, me + 3 < n)

    @pl.when(jnp.logical_not(straight))
    def _():
        clear(dv_buf[7])
        clear(dk_buf[7])

    def remote(src, dst, ss, rs, peer):
        return pltpu.make_async_remote_copy(
            src_ref=src, dst_ref=dst, send_sem=ss, recv_sem=rs,
            device_id={"ctx": peer}, device_id_type=pl.DeviceIdType.MESH,
        )

    def lanes(g, width):
        return pl.ds(pl.multiple_of(g * width, width), width)

    def head(win, at, g):
        return win.at[at, :, lanes(g, HEAD_SIZE)]

    def near(win, ss, rs, g):
        return remote(head(win, 0, g), head(win, 1, g), ss.at[0, g], rs.at[0, g], partner)

    def across(win, ss, rs, g):
        return remote(head(win, 0, g), head(win, 2, g), ss.at[1, g], rs.at[1, g], lax.rem(me + 2, n))

    def far(win, ss, rs, g):
        return remote(head(win, 0, g), head(win, 3, g), ss.at[2, g], rs.at[2, g], lax.rem(me + 3, n))

    def pass_on(win, ss, rs, g):
        at = 3 - 2 * odd
        return remote(head(win, 2, g), head(win, at, g), ss.at[3, g], rs.at[at - 1, g], partner)

    far_too = jnp.logical_and(odd == 1, me + 3 < n)

    def spread(win, ss, rs, g):
        @pl.when(me + 2 < n)
        def _():
            across(win, ss, rs, g).start()

        @pl.when(far_too)
        def _():
            far(win, ss, rs, g).start()

        @pl.when(odd == 0)
        def _():
            near(win, ss, rs, g).start()

    def relay(win, ss, rs, g):
        @pl.when(me >= 2)
        def _():
            across(win, ss, rs, g).wait_recv()
            pass_on(win, ss, rs, g).start()

    def settle(win, ss, rs, g):
        @pl.when(me >= 1)
        def _():
            near(win, ss, rs, g).wait_recv()

        @pl.when(me >= 3)
        def _():
            far(win, ss, rs, g).wait_recv()

    def spread_sent(win, ss, rs, g):
        @pl.when(me + 2 < n)
        def _():
            across(win, ss, rs, g).wait_send()

        @pl.when(far_too)
        def _():
            far(win, ss, rs, g).wait_send()

        @pl.when(odd == 0)
        def _():
            near(win, ss, rs, g).wait_send()

        @pl.when(me >= 2)
        def _():
            pass_on(win, ss, rs, g).wait_send()

    def meet(buf, ss, rs, g):
        return remote(buf[2].at[g], buf[5].at[g], ss.at[0, g], rs.at[0, g], partner)

    def back(buf, ss, rs, g):
        return remote(buf[4].at[g], buf[6].at[g], ss.at[1, g], rs.at[1, g], lax.rem(me + n - 2, n))

    def direct(buf, ss, rs, g):
        return remote(buf[3].at[g], buf[7].at[g], ss.at[2, g], rs.at[2, g], lax.rem(me + n - 3 + 2 * odd, n))

    has_direct = jnp.logical_or(odd == 1, me >= 3)

    def send_terms(buf, ss, rs, g, terms):
        own, mid = buf[0], buf[1]
        one, two, three = (terms[d * TILE:(d + 1) * TILE] for d in (1, 2, 3))
        own[g] = terms[0:TILE]
        mid[g] = two
        buf[2][g] = jnp.where(odd == 1, three, one).astype(BF16)
        buf[3][g] = jnp.where(odd == 1, one, three).astype(BF16)

        @pl.when(me >= 2)
        def _():
            meet(buf, ss, rs, g).start()

        @pl.when(has_direct)
        def _():
            direct(buf, ss, rs, g).start()

    def finish_terms(buf, ss, rs, g):
        meet(buf, ss, rs, g).wait_recv()
        buf[4][g] = (buf[1][g] + buf[5][g].astype(F32)).astype(BF16)
        back(buf, ss, rs, g).start()

    def gather_back(buf, out, ss, rs):
        for g in range(groups):
            @pl.when(straight)
            def _():
                direct(buf, ss, rs, g).wait_recv()

            @pl.when(me + 2 < n)
            def _():
                back(buf, ss, rs, g).wait_recv()

            acc = buf[0][g] + buf[6][g].astype(F32) + buf[7][g].astype(F32)
            out[:, g * HEAD_SIZE:(g + 1) * HEAD_SIZE] = acc.astype(BF16)

    def terms_sent(buf, ss, rs):
        for g in range(groups):
            @pl.when(me >= 2)
            def _():
                meet(buf, ss, rs, g).wait_send()
                back(buf, ss, rs, g).wait_send()

            @pl.when(has_direct)
            def _():
                direct(buf, ss, rs, g).wait_send()

    def low_copy(d):
        return remote(lwin.at[0], lwin.at[d], l_s.at[d - 1], l_r.at[d - 1], lax.rem(me + d, n))

    def rows(j):
        return pl.ds(pl.multiple_of(j * R, R), R)

    def scatter(src, dst, peer, ss, rs):
        return pltpu.make_async_remote_copy(
            src_ref=src.at[rows(peer)], dst_ref=dst.at[rows(me)], send_sem=ss.at[peer], recv_sem=rs.at[me],
            device_id={"ctx": peer}, device_id_type=pl.DeviceIdType.MESH,
        )

    def arrived(dst, source, ss, rs):
        return pltpu.make_async_remote_copy(
            src_ref=dst.at[rows(source)], dst_ref=dst.at[rows(source)], send_sem=ss.at[source],
            recv_sem=rs.at[source], device_id={"ctx": source}, device_id_type=pl.DeviceIdType.MESH,
        )

    def wait_arrivals(dst, ss, rs):
        def one(i, carry):
            arrived(dst, lax.rem(me + i, n), ss, rs).wait_recv()
            return carry

        lax.fori_loop(1, n, one, 0)

    def wait_sends(src, dst, ss, rs):
        def one(i, carry):
            scatter(src, dst, lax.rem(me + i, n), ss, rs).wait_send()
            return carry

        lax.fori_loop(1, n, one, 0)

    row_id = lax.broadcasted_iota(jnp.int32, (R, up_lanes), 0)

    def factors(j):
        tenant = ten[j]
        row = upf[pl.ds(tenant, 1), :]
        tail = jnp.zeros((R, up_lanes), F32)
        for k in range(up_rows):
            tail = jnp.where(row_id == k, row[:, k * up_lanes:(k + 1) * up_lanes], tail)
        return down[tenant], tail.astype(BF16)

    def prepare(i, carry):
        peer = lax.rem(me + i, n)
        mat, tail = factors(peer)
        send_a[rows(peer), 0:piece] = mat
        send_a[rows(peer), piece:piece + up_lanes] = tail
        return carry

    def give(i, carry):
        scatter(send_a, recv_a, lax.rem(me + i, n), a_s, a_r).start()
        return carry

    loads[1].wait()
    lax.fori_loop(1, n, prepare, 0)
    loads[0].wait()
    pl.semaphore_wait(barrier, n - 1)
    for g in range(groups):
        spread(kwin, k_s, k_r, g)
    mat, tail = factors(me)
    recv_a[rows(me), 0:piece] = mat
    recv_a[rows(me), piece:piece + up_lanes] = tail

    col = lax.broadcasted_iota(jnp.int32, (1, n * R), 1)
    col_tile = jnp.right_shift(col, 4)
    col_rank = jnp.bitwise_and(col, R - 1)
    col_tenant = jnp.zeros((1, n * R), jnp.int32)
    for j in range(n):
        col_tenant = jnp.where(col_tile == j, ten[j], col_tenant)
    blocks = adapters // 16
    for b in range(blocks):
        line = lax.broadcasted_iota(jnp.int32, (16 * R, n * R), 0)
        hit = jnp.logical_and(
            col_tenant == b * 16 + jnp.right_shift(line, 4), col_rank == jnp.bitwise_and(line, R - 1)
        )
        pick[b * 16 * R:(b + 1) * 16 * R, :] = jnp.where(hit, 1.0, 0.0).astype(BF16)

    loads[2].wait()
    loads[3].wait()
    for g in range(2):
        relay(kwin, k_s, k_r, g)
    lax.fori_loop(1, n, give, 0)
    loads[5].wait()
    for g in range(groups):
        spread(fwin, f_s, f_r, g)

    def stack(ref, g):
        part = ref[:, lanes(g, gw)]
        return jnp.concatenate([part[:, h * HEAD_SIZE:(h + 1) * HEAD_SIZE] for h in range(heads)], axis=0)

    def first(g, carry):
        settle(kwin, k_s, k_r, g)
        kg = kwin[:, :, lanes(g, HEAD_SIZE)].reshape(window, HEAD_SIZE)
        qg = q[:, lanes(g, gw)]
        for h in range(heads):
            s = dot_nt(kg, qg[:, h * HEAD_SIZE:(h + 1) * HEAD_SIZE])
            parts = [s[0:TILE] + tri[...]]
            for d in range(1, reach + 1):
                parts.append(s[d * TILE:(d + 1) * TILE] + bias[d])
            s = jnp.concatenate(parts, axis=0)
            top = jnp.max(s, axis=0, keepdims=True)
            e = jnp.exp2((s - top) * (scale * LOG2E))
            inv = 1.0 / jnp.sum(e, axis=0, keepdims=True)
            pbuf[g, :, h * HEAD_SIZE:(h + 1) * HEAD_SIZE] = (e * inv).astype(BF16)
        dv = dot(pbuf[g], stack(do, g))
        send_terms(dv_buf, dv_s, dv_r, g, dv)

        @pl.when(g + 2 < groups)
        def _():
            relay(kwin, k_s, k_r, jnp.minimum(g + 2, groups - 1))

        @pl.when(jnp.logical_and(g >= 1, me >= 2))
        def _():
            finish_terms(dv_buf, dv_s, dv_r, g - 1)
        return carry

    lax.fori_loop(0, groups, first, 0)

    @pl.when(me >= 2)
    def _():
        finish_terms(dv_buf, dv_s, dv_r, groups - 1)
    for g in range(groups):
        relay(fwin, f_s, f_r, g)

    loads[4].wait()
    wait_arrivals(recv_a, a_s, a_r)
    per = max(1, 512 // piece)
    low_t = jnp.zeros((R, TILE), F32)
    for c in range(0, n, per):
        mats = [recv_a[j * R:(j + 1) * R, 0:piece] for j in range(c, c + per)]
        mats = mats[0] if per == 1 else jnp.concatenate(mats, axis=1)
        low_t = low_t + dot_nt(mats, hidden[:, c * piece:(c + per) * piece])
    low_half = low_t.astype(BF16)
    rank = lax.broadcasted_iota(jnp.int32, (R, n * R), 0)
    ups = []
    for k in range(per_row):
        hit = jnp.logical_and(col_rank < up_rows, col_tile * up_rows + col_rank == rank * per_row + k)
        ups.append(dot(jnp.where(hit, 1.0, 0.0).astype(BF16), recv_a[:, piece:piece + up_lanes]))
    up = jnp.concatenate(ups, axis=1)
    up_half = up.astype(BF16)
    up_tall = jnp.concatenate([up, jnp.zeros((TILE - R, kvw), F32)], axis=0).astype(BF16)
    lwin[0] = low_half
    for d in range(1, reach + 1):
        @pl.when(me + d < n)
        def _():
            low_copy(d).start()

    gather_back(dv_buf, dv_ref, dv_s, dv_r)
    dv = dv_ref[...]
    grad_t = (ADAPTER_SCALE * dot_nt(up_half, dv)).astype(BF16)
    up_grad = ADAPTER_SCALE * dot(low_half, dv)
    for j in range(n):
        send_g[j * R:(j + 1) * R, 0:piece] = dot(grad_t, hidden[:, j * piece:(j + 1) * piece]).astype(BF16)
        tail = jnp.zeros((R, up_lanes), F32)
        for k in range(up_rows):
            r, c = divmod(j * up_rows + k, per_row)
            tail = jnp.where(row_id == k, up_grad[r:r + 1, c * up_lanes:(c + 1) * up_lanes], tail)
        send_g[j * R:(j + 1) * R, piece:piece + up_lanes] = tail.astype(BF16)

        @pl.when(me != j)
        def _():
            scatter(send_g, recv_g, j, g_s, g_r).start()

    recv_g[rows(me), :] = send_g[rows(me), :]

    for g in range(groups):
        settle(fwin, f_s, f_r, g)
    for d in range(1, reach + 1):
        @pl.when(me >= d)
        def _():
            low_copy(d).wait_recv()

    for d in range(reach + 1):
        low = jnp.concatenate([lwin[d].astype(F32), jnp.zeros((TILE - R, TILE), F32)], axis=0).T
        vwin[d] = (fwin[d].astype(F32) + ADAPTER_SCALE * dot(low.astype(BF16), up_tall)).astype(BF16)

    def dq_out(g):
        return pltpu.make_async_copy(dqv.at[g], dq_hbm.at[:, lanes(g, gw)], dq_sem.at[g])

    def second(g, carry):
        vg = vwin[:, :, lanes(g, HEAD_SIZE)].reshape(window, HEAD_SIZE)
        dog = do[:, lanes(g, gw)]
        for h in range(heads):
            at = slice(h * HEAD_SIZE, (h + 1) * HEAD_SIZE)
            dp = dot_nt(vg, dog[:, at])
            p = pbuf[g, :, at].astype(F32)
            delta = jnp.sum(p * dp, axis=0, keepdims=True)
            pbuf[g, :, at] = (p * ((dp - delta) * scale)).astype(BF16)
        dk = dot(pbuf[g], stack(q, g))
        send_terms(dk_buf, dk_s, dk_r, g, dk)

        @pl.when(jnp.logical_and(g >= 1, me >= 2))
        def _():
            finish_terms(dk_buf, dk_s, dk_r, g - 1)
        return carry

    lax.fori_loop(0, groups, second, 0)

    @pl.when(me >= 2)
    def _():
        finish_terms(dk_buf, dk_s, dk_r, groups - 1)

    def third(g, carry):
        kg = kwin[:, :, lanes(g, HEAD_SIZE)].reshape(window, HEAD_SIZE)
        dq_t = dot(kg.astype(F32).T.astype(BF16), pbuf[g])
        for h in range(heads):
            at = slice(h * HEAD_SIZE, (h + 1) * HEAD_SIZE)
            dqv[g, :, at] = dq_t[:, at].T.astype(BF16)
        dq_out(g).start()
        return carry

    lax.fori_loop(0, groups, third, 0)

    wait_arrivals(recv_g, g_s, g_r)
    line = lax.broadcasted_iota(jnp.int32, (16, n * R), 0)
    for b in range(blocks):
        out = dot(pick[b * 16 * R:(b + 1) * 16 * R, :], recv_g[:, 0:piece])
        gd_ref[b * 16:(b + 1) * 16] = out.reshape(16, R, piece)
        for k in range(up_rows):
            hit = jnp.logical_and(col_tenant == b * 16 + line, col_rank == k)
            gu_ref[b * 16:(b + 1) * 16, k * up_lanes:(k + 1) * up_lanes] = dot(
                jnp.where(hit, 1.0, 0.0).astype(BF16), recv_g[:, piece:piece + up_lanes]
            )
    gather_back(dk_buf, dk_ref, dk_s, dk_r)

    for g in range(groups):
        dq_out(g).wait()
    for d in range(1, reach + 1):
        @pl.when(me + d < n)
        def _():
            low_copy(d).wait_send()
    for g in range(groups):
        spread_sent(kwin, k_s, k_r, g)
        spread_sent(fwin, f_s, f_r, g)
    terms_sent(dv_buf, dv_s, dv_r)
    terms_sent(dk_buf, dk_s, dk_r)
    wait_sends(send_a, recv_a, a_s, a_r)
    wait_sends(send_g, recv_g, g_s, g_r)


def flush(*refs):
    ins, outs, held, sems = refs[0:5], refs[5:10], refs[10:15], refs[15]
    loads = [pltpu.make_async_copy(ins[i], held[i], sems.at[i]) for i in range(5)]
    stores = [pltpu.make_async_copy(held[i], outs[i], sems.at[5 + i]) for i in range(5)]
    for load in loads:
        load.start()
    for load, store in zip(loads, stores):
        load.wait()
        store.start()
    for store in stores:
        store.wait()


def per_device(
    hidden_in, queries, keys, frozen_values, d_out, adapter_down, adapter_up, seg_tiles, seg_tenant
):
    n = lax.axis_size("ctx")
    row_count, d_model = hidden_in.shape
    reach = (SEGMAX - TILE) // row_count
    adapters, piece, _ = adapter_down.shape
    up_piece = adapter_up.shape[1]
    kvw = keys.shape[1]
    qw = queries.shape[1]
    groups = kvw // HEAD_SIZE
    gw = qw // groups
    window = (reach + 1) * row_count
    wide = piece + min(up_piece, 128)
    vmem = pl.BlockSpec(memory_space=pltpu.VMEM)
    hbm = pl.BlockSpec(memory_space=pltpu.HBM)
    anywhere = pl.BlockSpec(memory_space=pl.ANY)
    sem = pltpu.SemaphoreType.DMA
    block = (groups, row_count, HEAD_SIZE)
    terms = [pltpu.VMEM(block, F32)] * 2 + [pltpu.VMEM(block, BF16)] * 6
    a2a = pltpu.VMEM((n * R, wide), BF16)
    results = pl.pallas_call(
        functools.partial(kernel, n, reach),
        out_shape=(
            jax.ShapeDtypeStruct((row_count, qw), BF16),
            jax.ShapeDtypeStruct((row_count, kvw), BF16),
            jax.ShapeDtypeStruct((row_count, kvw), BF16),
            jax.ShapeDtypeStruct((adapters, R, piece), F32),
            jax.ShapeDtypeStruct((adapters, up_piece), F32),
        ),
        in_specs=[hbm] * 9,
        out_specs=(anywhere, vmem, vmem, vmem, vmem),
        scratch_shapes=[
            pltpu.SMEM(seg_tiles.shape, jnp.int32),
            pltpu.SMEM(seg_tenant.shape, jnp.int32),
            pltpu.VMEM((adapters, up_piece), BF16),
            pltpu.VMEM((row_count, d_model), BF16),
            pltpu.VMEM((row_count, qw), BF16),
            pltpu.VMEM((row_count, qw), BF16),
            pltpu.VMEM((adapters, R, piece), BF16),
            pltpu.VMEM((reach + 1, row_count, kvw), BF16),
            pltpu.VMEM((reach + 1, row_count, kvw), BF16),
            pltpu.VMEM((reach + 1, R, row_count), BF16),
            pltpu.VMEM((reach + 1, row_count, kvw), BF16),
            pltpu.VMEM((adapters, up_piece), F32),
            a2a,
            a2a,
            pltpu.VMEM((groups, window, gw), BF16),
            pltpu.VMEM((groups, row_count, gw), BF16),
            pltpu.VMEM((TILE, TILE), F32),
            terms, terms,
            a2a,
            a2a,
            pltpu.VMEM((adapters * R, n * R), BF16),
            pltpu.SMEM((n,), jnp.int32),
            sem((9,)),
            sem((groups,)),
            sem((4, groups)), sem((3, groups)), sem((4, groups)), sem((3, groups)),
            sem((3,)), sem((3,)),
            sem((n,)), sem((n,)),
            sem((3, groups)), sem((3, groups)),
            sem((3, groups)), sem((3, groups)),
            sem((n,)), sem((n,)),
        ],
        compiler_params=pltpu.CompilerParams(
            collective_id=0, has_side_effects=True, vmem_limit_bytes=64 * 1024 * 1024
        ),
    )(
        seg_tiles, seg_tenant, hidden_in, queries, keys, frozen_values, d_out,
        jnp.swapaxes(adapter_down, 1, 2), adapter_up,
    )
    d_queries, d_keys, d_values, grad_down, grad_up = pl.pallas_call(
        flush,
        out_shape=tuple(jax.ShapeDtypeStruct(x.shape, x.dtype) for x in results),
        in_specs=[anywhere] * 5,
        out_specs=(hbm,) * 5,
        scratch_shapes=[pltpu.VMEM(x.shape, x.dtype) for x in results] + [sem((10,))],
        compiler_params=pltpu.CompilerParams(vmem_limit_bytes=64 * 1024 * 1024),
    )(*results)
    return (d_queries, d_keys, d_values, jnp.swapaxes(grad_down, 1, 2), grad_up)


def solution(mesh):
    placed = (
        P(("groups", "ctx"), None),
        P(("groups", "ctx"), None),
        P(("groups", "ctx"), None),
        P(("groups", "ctx"), None),
        P(("groups", "ctx"), None),
        P(None, "ctx", None),
        P(None, "ctx"),
        P("groups"),
        P("groups"),
    )
    return jax.shard_map(
        per_device,
        mesh=mesh,
        in_specs=placed,
        out_specs=(
            P(("groups", "ctx"), None),
            P(("groups", "ctx"), None),
            P(("groups", "ctx"), None),
            P("groups", "ctx", None),
            P("groups", "ctx"),
        ),
        check_vma=False,
    )
```

```python
import functools

import jax
import jax.numpy as jnp
from jax import lax
from jax.experimental import pallas as pl
from jax.experimental.pallas import tpu as pltpu
from jax.sharding import PartitionSpec as P

HEAD_SIZE = 128
R = 16
TILE = 128
SEGMAX = 512
ADAPTER_SCALE = 2.0
NEG_BIG = -1e30
LOG2E = 1.4426950408889634
NT = (((1,), (1,)), ((), ()))
F32 = jnp.float32
BF16 = jnp.bfloat16


def dot(a, b):
    return jnp.dot(a, b, preferred_element_type=F32)


def dot_nt(a, b):
    return lax.dot_general(a, b, NT, preferred_element_type=F32)


def kernel(
    n, reach, tiles_hbm, tenant_hbm, hidden_hbm, q_hbm, keys_hbm, frozen_hbm, do_hbm, down_hbm, up_hbm,
    dq_hbm, dk_hbm, dv_hbm, gd_hbm, gu_hbm,
    dk_ref, dv_ref, gd_ref, gu_ref, out_sem,
    seg_tiles, seg_tenant, up_in, hidden, q, do, down, kwin, fwin, lwin, vwin, upf, send_a, recv_a, pbuf, dqv, tri,
    dv_buf, dk_buf, send_g, recv_g, pick, ten,
    load_sem, dq_sem, k_s, k_r, f_s, f_r, l_s, l_r, a_s, a_r, dv_s, dv_r, dk_s, dk_r, g_s, g_r,
):
    me = lax.axis_index("ctx")
    odd = lax.rem(me, 2)
    partner = me + 1 - 2 * odd
    adapters, _, piece = down.shape
    up_piece = upf.shape[1]
    up_lanes = min(up_piece, 128)
    up_rows = up_piece // up_lanes
    kvw = kwin.shape[2]
    groups = kvw // HEAD_SIZE
    gw = q.shape[1] // groups
    heads = gw // HEAD_SIZE
    per_row = kvw // up_lanes
    segs = seg_tiles.shape[0]
    window = (reach + 1) * TILE
    scale = HEAD_SIZE ** -0.5

    pairs = (
        (keys_hbm, kwin.at[0]), (down_hbm, down), (q_hbm, q), (do_hbm, do),
        (hidden_hbm, hidden), (frozen_hbm, fwin.at[0]),
        (tiles_hbm, seg_tiles), (tenant_hbm, seg_tenant), (up_hbm, up_in),
    )
    loads = [pltpu.make_async_copy(a, b, load_sem.at[i]) for i, (a, b) in enumerate(pairs)]
    for i in (6, 7, 0, 8, 1, 2, 3, 4, 5):
        loads[i].start()

    barrier = pltpu.get_barrier_semaphore()

    def greet(i, carry):
        pl.semaphore_signal(
            barrier, inc=1, device_id={"ctx": lax.rem(me + i, n)}, device_id_type=pl.DeviceIdType.MESH
        )
        return carry

    lax.fori_loop(1, n, greet, 0)

    loads[6].wait()
    loads[7].wait()
    ends = []
    total = jnp.int32(0)
    for i in range(segs):
        total = total + seg_tiles[i]
        ends.append(total)

    def segment(j):
        s = jnp.int32(0)
        for end in ends:
            s = s + (end <= j).astype(jnp.int32)
        return s

    def note(j, carry):
        ten[j] = seg_tenant[jnp.minimum(segment(j), segs - 1)]
        return carry

    lax.fori_loop(0, n, note, 0)
    my_segment = segment(me)
    bias = [None]
    for d in range(1, reach + 1):
        same = jnp.logical_and(me >= d, segment(me - d) == my_segment)
        bias.append(jnp.where(same, jnp.float32(0), jnp.float32(NEG_BIG)))
    w_place = lax.broadcasted_iota(jnp.int32, (TILE, TILE), 0)
    t_place = lax.broadcasted_iota(jnp.int32, (TILE, TILE), 1)
    tri[...] = jnp.where(w_place <= t_place, 0.0, NEG_BIG).astype(F32)
    loads[8].wait()
    upf[...] = up_in[...].astype(F32)

    for d in range(1, reach + 1):
        @pl.when(me < d)
        def _():
            kwin[d] = jnp.zeros((TILE, kvw), BF16)
            fwin[d] = jnp.zeros((TILE, kvw), BF16)
            lwin[d] = jnp.zeros((R, TILE), BF16)

    def clear(ref):
        ref[...] = jnp.zeros(ref.shape, ref.dtype)

    @pl.when(me + 2 >= n)
    def _():
        clear(dv_buf[6])
        clear(dk_buf[6])

    straight = jnp.logical_or(odd == 0, me + 3 < n)

    @pl.when(jnp.logical_not(straight))
    def _():
        clear(dv_buf[7])
        clear(dk_buf[7])

    def remote(src, dst, ss, rs, peer):
        return pltpu.make_async_remote_copy(
            src_ref=src, dst_ref=dst, send_sem=ss, recv_sem=rs,
            device_id={"ctx": peer}, device_id_type=pl.DeviceIdType.MESH,
        )

    def lanes(g, width):
        return pl.ds(pl.multiple_of(g * width, width), width)

    def head(win, at, g):
        return win.at[at, :, lanes(g, HEAD_SIZE)]

    def near(win, ss, rs, g):
        return remote(head(win, 0, g), head(win, 1, g), ss.at[0, g], rs.at[0, g], partner)

    def across(win, ss, rs, g):
        return remote(head(win, 0, g), head(win, 2, g), ss.at[1, g], rs.at[1, g], lax.rem(me + 2, n))

    def far(win, ss, rs, g):
        return remote(head(win, 0, g), head(win, 3, g), ss.at[2, g], rs.at[2, g], lax.rem(me + 3, n))

    def pass_on(win, ss, rs, g):
        at = 3 - 2 * odd
        return remote(head(win, 2, g), head(win, at, g), ss.at[3, g], rs.at[at - 1, g], partner)

    far_too = jnp.logical_and(odd == 1, me + 3 < n)

    def spread(win, ss, rs, g):
        @pl.when(me + 2 < n)
        def _():
            across(win, ss, rs, g).start()

        @pl.when(far_too)
        def _():
            far(win, ss, rs, g).start()

        @pl.when(odd == 0)
        def _():
            near(win, ss, rs, g).start()

    def relay(win, ss, rs, g):
        @pl.when(me >= 2)
        def _():
            across(win, ss, rs, g).wait_recv()
            pass_on(win, ss, rs, g).start()

    def settle(win, ss, rs, g):
        @pl.when(me >= 1)
        def _():
            near(win, ss, rs, g).wait_recv()

        @pl.when(me >= 3)
        def _():
            far(win, ss, rs, g).wait_recv()

    def spread_sent(win, ss, rs, g):
        @pl.when(me + 2 < n)
        def _():
            across(win, ss, rs, g).wait_send()

        @pl.when(far_too)
        def _():
            far(win, ss, rs, g).wait_send()

        @pl.when(odd == 0)
        def _():
            near(win, ss, rs, g).wait_send()

        @pl.when(me >= 2)
        def _():
            pass_on(win, ss, rs, g).wait_send()

    def meet(buf, ss, rs, g):
        return remote(buf[2].at[g], buf[5].at[g], ss.at[0, g], rs.at[0, g], partner)

    def back(buf, ss, rs, g):
        return remote(buf[4].at[g], buf[6].at[g], ss.at[1, g], rs.at[1, g], lax.rem(me + n - 2, n))

    def direct(buf, ss, rs, g):
        return remote(buf[3].at[g], buf[7].at[g], ss.at[2, g], rs.at[2, g], lax.rem(me + n - 3 + 2 * odd, n))

    has_direct = jnp.logical_or(odd == 1, me >= 3)

    def send_terms(buf, ss, rs, g, terms):
        own, mid = buf[0], buf[1]
        one, two, three = (terms[d * TILE:(d + 1) * TILE] for d in (1, 2, 3))
        own[g] = terms[0:TILE]
        mid[g] = two
        buf[2][g] = jnp.where(odd == 1, three, one).astype(BF16)
        buf[3][g] = jnp.where(odd == 1, one, three).astype(BF16)

        @pl.when(me >= 2)
        def _():
            meet(buf, ss, rs, g).start()

        @pl.when(has_direct)
        def _():
            direct(buf, ss, rs, g).start()

    def finish_terms(buf, ss, rs, g):
        meet(buf, ss, rs, g).wait_recv()
        buf[4][g] = (buf[1][g] + buf[5][g].astype(F32)).astype(BF16)
        back(buf, ss, rs, g).start()

    def gather_back(buf, out, ss, rs):
        for g in range(groups):
            @pl.when(straight)
            def _():
                direct(buf, ss, rs, g).wait_recv()

            @pl.when(me + 2 < n)
            def _():
                back(buf, ss, rs, g).wait_recv()

            acc = buf[0][g] + buf[6][g].astype(F32) + buf[7][g].astype(F32)
            out[:, g * HEAD_SIZE:(g + 1) * HEAD_SIZE] = acc.astype(BF16)

    def terms_sent(buf, ss, rs):
        for g in range(groups):
            @pl.when(me >= 2)
            def _():
                meet(buf, ss, rs, g).wait_send()
                back(buf, ss, rs, g).wait_send()

            @pl.when(has_direct)
            def _():
                direct(buf, ss, rs, g).wait_send()

    def low_copy(d):
        return remote(lwin.at[0], lwin.at[d], l_s.at[d - 1], l_r.at[d - 1], lax.rem(me + d, n))

    def rows(j):
        return pl.ds(pl.multiple_of(j * R, R), R)

    def scatter(src, dst, peer, ss, rs):
        return pltpu.make_async_remote_copy(
            src_ref=src.at[rows(peer)], dst_ref=dst.at[rows(me)], send_sem=ss.at[peer], recv_sem=rs.at[me],
            device_id={"ctx": peer}, device_id_type=pl.DeviceIdType.MESH,
        )

    def arrived(dst, source, ss, rs):
        return pltpu.make_async_remote_copy(
            src_ref=dst.at[rows(source)], dst_ref=dst.at[rows(source)], send_sem=ss.at[source],
            recv_sem=rs.at[source], device_id={"ctx": source}, device_id_type=pl.DeviceIdType.MESH,
        )

    def wait_arrivals(dst, ss, rs):
        def one(i, carry):
            arrived(dst, lax.rem(me + i, n), ss, rs).wait_recv()
            return carry

        lax.fori_loop(1, n, one, 0)

    def wait_sends(src, dst, ss, rs):
        def one(i, carry):
            scatter(src, dst, lax.rem(me + i, n), ss, rs).wait_send()
            return carry

        lax.fori_loop(1, n, one, 0)

    row_id = lax.broadcasted_iota(jnp.int32, (R, up_lanes), 0)

    def factors(j):
        tenant = ten[j]
        row = upf[pl.ds(tenant, 1), :]
        tail = jnp.zeros((R, up_lanes), F32)
        for k in range(up_rows):
            tail = jnp.where(row_id == k, row[:, k * up_lanes:(k + 1) * up_lanes], tail)
        return down[tenant], tail.astype(BF16)

    def prepare(i, carry):
        peer = lax.rem(me + i, n)
        mat, tail = factors(peer)
        send_a[rows(peer), 0:piece] = mat
        send_a[rows(peer), piece:piece + up_lanes] = tail
        return carry

    def give(i, carry):
        scatter(send_a, recv_a, lax.rem(me + i, n), a_s, a_r).start()
        return carry

    loads[1].wait()
    lax.fori_loop(1, n, prepare, 0)
    loads[0].wait()
    pl.semaphore_wait(barrier, n - 1)
    for g in range(groups):
        spread(kwin, k_s, k_r, g)
    mat, tail = factors(me)
    recv_a[rows(me), 0:piece] = mat
    recv_a[rows(me), piece:piece + up_lanes] = tail

    col = lax.broadcasted_iota(jnp.int32, (1, n * R), 1)
    col_tile = jnp.right_shift(col, 4)
    col_rank = jnp.bitwise_and(col, R - 1)
    col_tenant = jnp.zeros((1, n * R), jnp.int32)
    for j in range(n):
        col_tenant = jnp.where(col_tile == j, ten[j], col_tenant)
    blocks = adapters // 16
    for b in range(blocks):
        line = lax.broadcasted_iota(jnp.int32, (16 * R, n * R), 0)
        hit = jnp.logical_and(
            col_tenant == b * 16 + jnp.right_shift(line, 4), col_rank == jnp.bitwise_and(line, R - 1)
        )
        pick[b * 16 * R:(b + 1) * 16 * R, :] = jnp.where(hit, 1.0, 0.0).astype(BF16)

    loads[2].wait()
    loads[3].wait()
    for g in range(2):
        relay(kwin, k_s, k_r, g)
    lax.fori_loop(1, n, give, 0)
    loads[5].wait()
    for g in range(groups):
        spread(fwin, f_s, f_r, g)

    def stack(ref, g):
        part = ref[:, lanes(g, gw)]
        return jnp.concatenate([part[:, h * HEAD_SIZE:(h + 1) * HEAD_SIZE] for h in range(heads)], axis=0)

    def first(g, carry):
        settle(kwin, k_s, k_r, g)
        kg = kwin[:, :, lanes(g, HEAD_SIZE)].reshape(window, HEAD_SIZE)
        qg = q[:, lanes(g, gw)]
        for h in range(heads):
            s = dot_nt(kg, qg[:, h * HEAD_SIZE:(h + 1) * HEAD_SIZE])
            parts = [s[0:TILE] + tri[...]]
            for d in range(1, reach + 1):
                parts.append(s[d * TILE:(d + 1) * TILE] + bias[d])
            s = jnp.concatenate(parts, axis=0)
            top = jnp.max(s, axis=0, keepdims=True)
            e = jnp.exp2((s - top) * (scale * LOG2E))
            inv = 1.0 / jnp.sum(e, axis=0, keepdims=True)
            pbuf[g, :, h * HEAD_SIZE:(h + 1) * HEAD_SIZE] = (e * inv).astype(BF16)
        dv = dot(pbuf[g], stack(do, g))
        send_terms(dv_buf, dv_s, dv_r, g, dv)

        @pl.when(g + 2 < groups)
        def _():
            relay(kwin, k_s, k_r, jnp.minimum(g + 2, groups - 1))

        @pl.when(jnp.logical_and(g >= 1, me >= 2))
        def _():
            finish_terms(dv_buf, dv_s, dv_r, g - 1)
        return carry

    lax.fori_loop(0, groups, first, 0)

    @pl.when(me >= 2)
    def _():
        finish_terms(dv_buf, dv_s, dv_r, groups - 1)
    for g in range(groups):
        relay(fwin, f_s, f_r, g)

    loads[4].wait()
    wait_arrivals(recv_a, a_s, a_r)
    per = max(1, 512 // piece)
    low_t = jnp.zeros((R, TILE), F32)
    for c in range(0, n, per):
        mats = [recv_a[j * R:(j + 1) * R, 0:piece] for j in range(c, c + per)]
        mats = mats[0] if per == 1 else jnp.concatenate(mats, axis=1)
        low_t = low_t + dot_nt(mats, hidden[:, c * piece:(c + per) * piece])
    low_half = low_t.astype(BF16)
    rank = lax.broadcasted_iota(jnp.int32, (R, n * R), 0)
    ups = []
    for k in range(per_row):
        hit = jnp.logical_and(col_rank < up_rows, col_tile * up_rows + col_rank == rank * per_row + k)
        ups.append(dot(jnp.where(hit, 1.0, 0.0).astype(BF16), recv_a[:, piece:piece + up_lanes]))
    up = jnp.concatenate(ups, axis=1)
    up_half = up.astype(BF16)
    up_tall = jnp.concatenate([up, jnp.zeros((TILE - R, kvw), F32)], axis=0).astype(BF16)
    lwin[0] = low_half
    for d in range(1, reach + 1):
        @pl.when(me + d < n)
        def _():
            low_copy(d).start()

    outs = [
        pltpu.make_async_copy(a, b, out_sem.at[i])
        for i, (a, b) in enumerate(((dv_ref, dv_hbm), (gd_ref, gd_hbm), (gu_ref, gu_hbm), (dk_ref, dk_hbm)))
    ]
    gather_back(dv_buf, dv_ref, dv_s, dv_r)
    outs[0].start()
    dv = dv_ref[...]
    grad_t = (ADAPTER_SCALE * dot_nt(up_half, dv)).astype(BF16)
    up_grad = ADAPTER_SCALE * dot(low_half, dv)
    for j in range(n):
        send_g[j * R:(j + 1) * R, 0:piece] = dot(grad_t, hidden[:, j * piece:(j + 1) * piece]).astype(BF16)
        tail = jnp.zeros((R, up_lanes), F32)
        for k in range(up_rows):
            r, c = divmod(j * up_rows + k, per_row)
            tail = jnp.where(row_id == k, up_grad[r:r + 1, c * up_lanes:(c + 1) * up_lanes], tail)
        send_g[j * R:(j + 1) * R, piece:piece + up_lanes] = tail.astype(BF16)

        @pl.when(me != j)
        def _():
            scatter(send_g, recv_g, j, g_s, g_r).start()

    recv_g[rows(me), :] = send_g[rows(me), :]

    for g in range(groups):
        settle(fwin, f_s, f_r, g)
    for d in range(1, reach + 1):
        @pl.when(me >= d)
        def _():
            low_copy(d).wait_recv()

    for d in range(reach + 1):
        low = jnp.concatenate([lwin[d].astype(F32), jnp.zeros((TILE - R, TILE), F32)], axis=0).T
        vwin[d] = (fwin[d].astype(F32) + ADAPTER_SCALE * dot(low.astype(BF16), up_tall)).astype(BF16)

    def dq_out(g):
        return pltpu.make_async_copy(dqv.at[g], dq_hbm.at[:, lanes(g, gw)], dq_sem.at[g])

    def second(g, carry):
        vg = vwin[:, :, lanes(g, HEAD_SIZE)].reshape(window, HEAD_SIZE)
        dog = do[:, lanes(g, gw)]
        for h in range(heads):
            at = slice(h * HEAD_SIZE, (h + 1) * HEAD_SIZE)
            dp = dot_nt(vg, dog[:, at])
            p = pbuf[g, :, at].astype(F32)
            delta = jnp.sum(p * dp, axis=0, keepdims=True)
            pbuf[g, :, at] = (p * ((dp - delta) * scale)).astype(BF16)
        dk = dot(pbuf[g], stack(q, g))
        send_terms(dk_buf, dk_s, dk_r, g, dk)

        @pl.when(jnp.logical_and(g >= 1, me >= 2))
        def _():
            finish_terms(dk_buf, dk_s, dk_r, g - 1)
        return carry

    lax.fori_loop(0, groups, second, 0)

    @pl.when(me >= 2)
    def _():
        finish_terms(dk_buf, dk_s, dk_r, groups - 1)

    def third(g, carry):
        kg = kwin[:, :, lanes(g, HEAD_SIZE)].reshape(window, HEAD_SIZE)
        dq_t = dot(kg.astype(F32).T.astype(BF16), pbuf[g])
        for h in range(heads):
            at = slice(h * HEAD_SIZE, (h + 1) * HEAD_SIZE)
            dqv[g, :, at] = dq_t[:, at].T.astype(BF16)
        dq_out(g).start()
        return carry

    lax.fori_loop(0, groups, third, 0)

    wait_arrivals(recv_g, g_s, g_r)
    line = lax.broadcasted_iota(jnp.int32, (16, n * R), 0)
    for b in range(blocks):
        out = dot(pick[b * 16 * R:(b + 1) * 16 * R, :], recv_g[:, 0:piece])
        gd_ref[b * 16:(b + 1) * 16] = out.reshape(16, R, piece)
        for k in range(up_rows):
            hit = jnp.logical_and(col_tenant == b * 16 + line, col_rank == k)
            gu_ref[b * 16:(b + 1) * 16, k * up_lanes:(k + 1) * up_lanes] = dot(
                jnp.where(hit, 1.0, 0.0).astype(BF16), recv_g[:, piece:piece + up_lanes]
            )
    outs[1].start()
    outs[2].start()
    gather_back(dk_buf, dk_ref, dk_s, dk_r)
    outs[3].start()

    for g in range(groups):
        dq_out(g).wait()
    for d in range(1, reach + 1):
        @pl.when(me + d < n)
        def _():
            low_copy(d).wait_send()
    for g in range(groups):
        spread_sent(kwin, k_s, k_r, g)
        spread_sent(fwin, f_s, f_r, g)
    terms_sent(dv_buf, dv_s, dv_r)
    terms_sent(dk_buf, dk_s, dk_r)
    wait_sends(send_a, recv_a, a_s, a_r)
    wait_sends(send_g, recv_g, g_s, g_r)
    for out in outs:
        out.wait()


def flush(*refs):
    ins, outs, held, sems = refs[0:5], refs[5:10], refs[10:15], refs[15]
    loads = [pltpu.make_async_copy(ins[i], held[i], sems.at[i]) for i in range(5)]
    stores = [pltpu.make_async_copy(held[i], outs[i], sems.at[5 + i]) for i in range(5)]
    for load in loads:
        load.start()
    for load, store in zip(loads, stores):
        load.wait()
        store.start()
    for store in stores:
        store.wait()


def per_device(
    hidden_in, queries, keys, frozen_values, d_out, adapter_down, adapter_up, seg_tiles, seg_tenant
):
    n = lax.axis_size("ctx")
    row_count, d_model = hidden_in.shape
    reach = (SEGMAX - TILE) // row_count
    adapters, piece, _ = adapter_down.shape
    up_piece = adapter_up.shape[1]
    kvw = keys.shape[1]
    qw = queries.shape[1]
    groups = kvw // HEAD_SIZE
    gw = qw // groups
    window = (reach + 1) * row_count
    wide = piece + min(up_piece, 128)
    hbm = pl.BlockSpec(memory_space=pltpu.HBM)
    anywhere = pl.BlockSpec(memory_space=pl.ANY)
    sem = pltpu.SemaphoreType.DMA
    block = (groups, row_count, HEAD_SIZE)
    terms = [pltpu.VMEM(block, F32)] * 2 + [pltpu.VMEM(block, BF16)] * 6
    a2a = pltpu.VMEM((n * R, wide), BF16)
    results = pl.pallas_call(
        functools.partial(kernel, n, reach),
        out_shape=(
            jax.ShapeDtypeStruct((row_count, qw), BF16),
            jax.ShapeDtypeStruct((row_count, kvw), BF16),
            jax.ShapeDtypeStruct((row_count, kvw), BF16),
            jax.ShapeDtypeStruct((adapters, R, piece), F32),
            jax.ShapeDtypeStruct((adapters, up_piece), F32),
        ),
        in_specs=[hbm] * 9,
        out_specs=(hbm,) * 5,
        scratch_shapes=[
            pltpu.VMEM((row_count, kvw), BF16),
            pltpu.VMEM((row_count, kvw), BF16),
            pltpu.VMEM((adapters, R, piece), F32),
            pltpu.VMEM((adapters, up_piece), F32),
            sem((4,)),
            pltpu.SMEM(seg_tiles.shape, jnp.int32),
            pltpu.SMEM(seg_tenant.shape, jnp.int32),
            pltpu.VMEM((adapters, up_piece), BF16),
            pltpu.VMEM((row_count, d_model), BF16),
            pltpu.VMEM((row_count, qw), BF16),
            pltpu.VMEM((row_count, qw), BF16),
            pltpu.VMEM((adapters, R, piece), BF16),
            pltpu.VMEM((reach + 1, row_count, kvw), BF16),
            pltpu.VMEM((reach + 1, row_count, kvw), BF16),
            pltpu.VMEM((reach + 1, R, row_count), BF16),
            pltpu.VMEM((reach + 1, row_count, kvw), BF16),
            pltpu.VMEM((adapters, up_piece), F32),
            a2a,
            a2a,
            pltpu.VMEM((groups, window, gw), BF16),
            pltpu.VMEM((groups, row_count, gw), BF16),
            pltpu.VMEM((TILE, TILE), F32),
            terms, terms,
            a2a,
            a2a,
            pltpu.VMEM((adapters * R, n * R), BF16),
            pltpu.SMEM((n,), jnp.int32),
            sem((9,)),
            sem((groups,)),
            sem((4, groups)), sem((3, groups)), sem((4, groups)), sem((3, groups)),
            sem((3,)), sem((3,)),
            sem((n,)), sem((n,)),
            sem((3, groups)), sem((3, groups)),
            sem((3, groups)), sem((3, groups)),
            sem((n,)), sem((n,)),
        ],
        compiler_params=pltpu.CompilerParams(
            collective_id=0, has_side_effects=True, vmem_limit_bytes=64 * 1024 * 1024
        ),
    )(
        seg_tiles, seg_tenant, hidden_in, queries, keys, frozen_values, d_out,
        jnp.swapaxes(adapter_down, 1, 2), adapter_up,
    )
    d_queries, d_keys, d_values, grad_down, grad_up = pl.pallas_call(
        flush,
        out_shape=tuple(jax.ShapeDtypeStruct(x.shape, x.dtype) for x in results),
        in_specs=[anywhere] * 5,
        out_specs=(hbm,) * 5,
        scratch_shapes=[pltpu.VMEM(x.shape, x.dtype) for x in results] + [sem((10,))],
        compiler_params=pltpu.CompilerParams(vmem_limit_bytes=64 * 1024 * 1024),
    )(*results)
    return (d_queries, d_keys, d_values, jnp.swapaxes(grad_down, 1, 2), grad_up)


def solution(mesh):
    placed = (
        P(("groups", "ctx"), None),
        P(("groups", "ctx"), None),
        P(("groups", "ctx"), None),
        P(("groups", "ctx"), None),
        P(("groups", "ctx"), None),
        P(None, "ctx", None),
        P(None, "ctx"),
        P("groups"),
        P("groups"),
    )
    return jax.shard_map(
        per_device,
        mesh=mesh,
        in_specs=placed,
        out_specs=(
            P(("groups", "ctx"), None),
            P(("groups", "ctx"), None),
            P(("groups", "ctx"), None),
            P("groups", "ctx", None),
            P("groups", "ctx"),
        ),
        check_vma=False,
    )
```
